256 devices in a mesh: member: 16 (over y, z_hi), tensor: 16 (over z_lo, x, core).
Axes of the slice: x: 4, y: 4, z: 8 (z_hi: 4, z_lo: 2; z = z_hi * 2 + z_lo), core: 2. Of those that a mesh axis runs over, the one named last changes fastest.
Arguments:
- normed: bfloat16 [1024, 5120], P('tensor', 'member'), may hold values from -6 to 6
- base_gate: bfloat16 [5120, 16384], P('member', 'tensor'), may hold values from -0.078125 to 0.078125
- base_up: bfloat16 [5120, 16384], P('member', 'tensor'), may hold values from -0.078125 to 0.078125
- base_down: bfloat16 [16384, 5120], P('tensor', 'member'), may hold values from -0.046875 to 0.046875
- codes_gate: bfloat16 [20480, 16384], P('member', 'tensor'), may hold values from -4 to 4
- codes_up: bfloat16 [20480, 16384], P('member', 'tensor'), may hold values from -4 to 4
- codes_down: bfloat16 [16384, 20480], P('tensor', 'member'), may hold values from -4 to 4
- scale_gate: float32 [160, 128], P('member', 'tensor'), may hold values from 0.002 to 0.02
- scale_up: float32 [160, 128], P('member', 'tensor'), may hold values from 0.002 to 0.02
- scale_down: float32 [128, 160], P('tensor', 'member'), may hold values from 0.002 to 0.02
Outputs:
- mixed: bfloat16 [1024, 20480], P('tensor', 'member')
The draws below stay inside these ranges and needn't reach their ends.
All inputs are finite; a program needn't handle non-finite values.
Results may differ from the reference program's by a relative error of at most 0.023.
Values may be sent and summed in bfloat16 or wider, within the bound.
No kernel may reach another device: no remote copies, remote signals or barrier semaphores. Data moves between devices by JAX's collectives and lax.ppermute only.
A program may use at most 128 MiB of HBM per device.

```python
import math
import jax
import jax.numpy as jnp
from jax import lax

D = 5120
FF = 16384
MEMBERS = 4
QB = 128
TOKENS = 1024
BLOCK_ROWS = 1280
N_MEMBER = 16


def block_levels(stream_key, shape, pieces, least, high):
    def one(dim, blocks):
        heights = jax.random.uniform(jax.random.fold_in(jax.random.fold_in(stream_key, 6), dim), (blocks,), jnp.float32, least / len(pieces), high / len(pieces))
        return jnp.repeat(jnp.exp(heights), shape[dim] // blocks).reshape((-1,) + (1,) * (len(shape) - dim - 1))

    gain = one(*pieces[0])
    for cut in pieces[1:]:
        gain = gain * one(*cut)
    return gain


def scatter_about(key, dims, spread, limit, split=(), kind=jnp.bfloat16):
    drawn = spread * jax.random.normal(key, dims, jnp.float32)
    if split:
        drawn = drawn * block_levels(key, dims, split, -0.22, 0.18)
    return jnp.clip(drawn, -limit, limit).astype(kind)


def setup_inputs(seed: int = 0) -> dict:
    key_of = jax.random.split(jax.random.key(seed), 11)
    normed = scatter_about(key_of[0], (TOKENS, D), 1.0, 6.0, ((0, 16), (1, 16)))
    base_gate = scatter_about(key_of[1], (D, FF), D ** -0.5, 0.078125, ((0, 16), (1, 16)))
    base_up = scatter_about(key_of[2], (D, FF), D ** -0.5, 0.078125, ((0, 16), (1, 16)))
    base_down = scatter_about(key_of[3], (FF, D), FF ** -0.5, 0.046875, ((0, 16), (1, 16)))
    codes_gate = scatter_about(key_of[4], (MEMBERS * D, FF), 1.0, 4.0, ((0, 16), (1, 16)))
    codes_up = scatter_about(key_of[5], (MEMBERS * D, FF), 1.0, 4.0, ((0, 16), (1, 16)))
    codes_down = scatter_about(key_of[6], (FF, MEMBERS * D), 1.0, 4.0, ((0, 16), (1, 16)))
    scale_gate = jnp.clip(jnp.exp(math.log(0.02) - 2.30258502 * jax.random.uniform(key_of[7], (MEMBERS * D // QB, FF // QB), jnp.float32) ** block_levels(key_of[7], (MEMBERS * D // QB, FF // QB), ((0, 16), (1, 16)), -0.2, 0.2)), 0.002, 0.02)
    scale_up = jnp.clip(jnp.exp(math.log(0.02) - 2.30258502 * jax.random.uniform(key_of[8], (MEMBERS * D // QB, FF // QB), jnp.float32) ** block_levels(key_of[8], (MEMBERS * D // QB, FF // QB), ((0, 16), (1, 16)), -0.2, 0.2)), 0.002, 0.02)
    scale_down = jnp.clip(jnp.exp(math.log(0.02) - 2.30258502 * jax.random.uniform(key_of[9], (FF // QB, MEMBERS * D // QB), jnp.float32) ** block_levels(key_of[9], (FF // QB, MEMBERS * D // QB), ((0, 16), (1, 16)), -0.2, 0.2)), 0.002, 0.02)
    return {"normed": normed, "base_gate": base_gate, "base_up": base_up, "base_down": base_down, "codes_gate": codes_gate, "codes_up": codes_up, "codes_down": codes_down, "scale_gate": scale_gate, "scale_up": scale_up, "scale_down": scale_down}


def dequant(codes, scales, base):
    rows, cols = codes.shape
    blocks = codes.astype(jnp.float32).reshape(rows // QB, QB, cols // QB, QB) * scales[:, None, :, None]
    return (base.astype(jnp.float32) + blocks.reshape(rows, cols)).astype(jnp.bfloat16)


def reference(normed, base_gate, base_up, base_down, codes_gate, codes_up, codes_down, scale_gate, scale_up, scale_down):
    groups = N_MEMBER // MEMBERS

    def split_rows(array):
        return array.reshape(groups, MEMBERS, array.shape[0] // (groups * MEMBERS), array.shape[1])

    def split_cols(array):
        return array.reshape(array.shape[0], groups, MEMBERS, array.shape[1] // (groups * MEMBERS))

    gate_codes, up_codes, down_codes = split_rows(codes_gate), split_rows(codes_up), split_cols(codes_down)
    gate_scales, up_scales, down_scales = split_rows(scale_gate), split_rows(scale_up), split_cols(scale_down)

    def one_member(member):
        def pick_rows(array):
            chosen = lax.dynamic_index_in_dim(array, member, 1, keepdims=False)
            return chosen.reshape(-1, array.shape[3])

        def pick_cols(array):
            chosen = lax.dynamic_index_in_dim(array, member, 2, keepdims=False)
            return chosen.reshape(array.shape[0], -1)

        w_gate = dequant(pick_rows(gate_codes), pick_rows(gate_scales), base_gate)
        w_up = dequant(pick_rows(up_codes), pick_rows(up_scales), base_up)
        w_down = dequant(pick_cols(down_codes), pick_cols(down_scales), base_down)
        gate = jnp.dot(normed, w_gate, preferred_element_type=jnp.float32)
        up = jnp.dot(normed, w_up, preferred_element_type=jnp.float32)
        hidden = (jax.nn.silu(gate) * up).astype(jnp.bfloat16)
        return jnp.dot(hidden, w_down, preferred_element_type=jnp.float32).astype(jnp.bfloat16)

    outputs = lax.map(one_member, jnp.arange(MEMBERS, dtype=jnp.int32))
    outputs = outputs.reshape(MEMBERS, TOKENS, groups, BLOCK_ROWS).transpose(1, 2, 0, 3)
    return outputs.reshape(TOKENS, MEMBERS * D)
```

```python
import jax
import jax.numpy as jnp
from jax import lax
from jax.sharding import Mesh, PartitionSpec as P

QB = 128
BF = jnp.bfloat16
F32 = jnp.float32
Y, ZH, ZL, X, CORE = "y", "zh", "zl", "x", "core"
TENSOR = (ZL, X, CORE)


def dot(a, b):
    return jnp.dot(a, b, preferred_element_type=F32)


def shift(value, axis, step):
    size = lax.axis_size(axis)
    return lax.ppermute(value, axis, [(i, (i + step) % size) for i in range(size)])


def after(value, *earlier):
    return lax.optimization_barrier((value, *earlier))[0]


def dequant(codes, scales):
    rows, cols = codes.shape
    blocks = (
        codes.astype(F32).reshape(rows // QB, QB, cols // QB, QB) * scales[:, None, :, None]
    )
    return blocks.reshape(rows, cols).astype(BF)


def near(value, axis):
    return shift(value, axis, -1), shift(value, axis, 1)


def far(ahead, behind, axis):
    half = ahead.shape[0] // 2
    first = shift(behind[:half], axis, 1)
    second = shift(ahead[half:], axis, -1)
    return jnp.concatenate((first, second), 0)


def scatter_first(part, axis):
    opposite = part(2).astype(BF)
    half = opposite.shape[0] // 2
    sent = lax.optimization_barrier((opposite[:half], opposite[half:]))
    return sent, (shift(sent[0], axis, 1), shift(sent[1], axis, -1))


def scatter_second(part, got, axis):
    half = got[0].shape[0]
    ahead, behind = part(1), part(3)
    ahead = jnp.concatenate((ahead[:half] + got[0].astype(F32), ahead[half:]), 0).astype(BF)
    behind = jnp.concatenate((behind[:half], behind[half:] + got[1].astype(F32)), 0).astype(BF)
    return (ahead, behind), (shift(ahead, axis, 1), shift(behind, axis, -1))


def scatter_sum(part, got):
    return part(0) + got[0].astype(F32) + got[1].astype(F32)


def from_zero(pieces, me):
    return [lax.select_n((me * 3 + k) % 4, *pieces) for k in range(4)]


def local(
    normed,
    base_gate,
    base_up,
    base_down,
    codes_gate,
    codes_up,
    codes_down,
    scale_gate,
    scale_up,
    scale_down,
):
    y, zh = lax.axis_index(Y), lax.axis_index(ZH)

    own = normed.reshape(4, 1, 16, 320)
    feats = jnp.concatenate((own, shift(own, ZL, 1)), 1)
    ahead, behind = near(feats, ZH)
    opposite = shift(feats, ZH, 2)
    feats = jnp.concatenate((feats, ahead, opposite, behind), 3)
    gate_near = near(after(base_gate, ahead, behind), ZH)
    ahead, behind = near(feats, X)
    codes_up, codes_gate = after((codes_up, codes_gate), feats)
    first = shift(behind[:, :1], X, 1)
    second = shift(ahead[:, 1:], X, -1)
    feats = jnp.concatenate((feats, ahead, first, second, behind), 1)
    feats = jnp.concatenate((feats, shift(feats, CORE, 1)), 1)
    feats = lax.optimization_barrier(feats.reshape(1024, 1280))

    def rows_from_me(delta):
        delta = lax.optimization_barrier(delta)
        pieces = [
            lax.dynamic_slice_in_dim(delta, (zh + k) % 4 * 320, 320, 0) for k in range(4)
        ]
        return lax.optimization_barrier(jnp.concatenate(pieces, 0))

    def product(values, weight):
        def part(step):
            return dot(lax.dynamic_slice_in_dim(values, (y + step) % 4 * 256, 256, 0), weight)

        return part

    delta_up = rows_from_me(dequant(codes_up, scale_up))
    delta_gate = rows_from_me(dequant(codes_gate, scale_gate))
    base_term = product(feats[:, :320], base_up)
    base_sent, base_got = scatter_first(base_term, Y)
    feats = after(feats, base_sent)
    base_term = product(feats[:, :320], base_up)
    up_term = product(feats, delta_up)
    up_sent, up_got = scatter_first(up_term, Y)
    up_term = product(after(feats, up_sent), delta_up)

    base_got = after(base_got, up_sent)
    base_sent, base_got = scatter_second(base_term, base_got, Y)

    gate_near = after(gate_near, base_sent)
    gate_far = far(*gate_near, ZH)
    down_own = after(base_down.T, *gate_near)
    down_near = near(down_own, ZH)

    up_got = after(up_got, gate_near)
    up_sent, up_got = scatter_second(up_term, up_got, Y)

    base_got = after(base_got, up_sent)
    base_part = scatter_sum(base_term, base_got)

    def base_rows(step):
        return lax.dynamic_slice_in_dim(base_part, (zh + step) % 4 * 64, 64, 0)

    base_sent, base_got = scatter_first(base_rows, ZH)

    gate_far = after(gate_far, base_sent)
    gate_base = jnp.concatenate((base_gate, gate_near[0], gate_far, gate_near[1]), 0)
    w_gate = lax.optimization_barrier(delta_gate + gate_base)
    gate_term = product(feats, w_gate)
    gate_sent, gate_got = scatter_first(gate_term, Y)
    gate_term = product(after(feats, gate_sent), w_gate)
    up_got = after(up_got, gate_sent)

    base_got = after(base_got, gate_sent)
    base_sent, base_got = scatter_second(base_rows, base_got, ZH)
    codes_down = after(codes_down, base_sent)
    delta_down = rows_from_me(dequant(codes_down, scale_down).T)

    gate_got = after(gate_got, base_sent)
    gate_sent, gate_got = scatter_second(gate_term, gate_got, Y)

    base_got = after(base_got, gate_sent)
    mine = scatter_sum(base_rows, base_got).astype(BF)
    ahead, behind = near(mine, ZH)
    up = lax.optimization_barrier(scatter_sum(up_term, up_got))
    ahead, behind = after((ahead, behind), up)
    opposite = far(ahead, behind, ZH)

    down_near = after(down_near, ahead)
    down_far = far(*down_near, ZH)

    base_part = jnp.concatenate(from_zero((mine, ahead, opposite, behind), zh), 0)
    up = lax.optimization_barrier(up + base_part.astype(F32))
    gate_got = after(gate_got, up, *down_near)
    gate = scatter_sum(gate_term, gate_got)
    hidden = (jax.nn.silu(gate) * up).astype(BF)
    ahead, behind = near(hidden, Y)
    pieces = (hidden, ahead, far(ahead, behind, Y), behind)

    down_far = after(down_far, ahead, behind)
    down_base = jnp.concatenate((down_own, down_near[0], down_far, down_near[1]), 0)
    w_down = lax.optimization_barrier(delta_down + down_base)

    def down(half):
        rows = jnp.concatenate([p[half * 128 : half * 128 + 128] for p in pieces], 0)
        return lax.dot_general(rows, w_down, (((1,), (1,)), ((), ())), preferred_element_type=F32)

    other = shift(down(1).astype(BF), CORE, 1)
    whole = lax.optimization_barrier((down(0) + other.astype(F32)).astype(BF))
    whole = whole.reshape(4, 4, 2, 16, 1280)

    def for_x(step):
        return whole[:, step].transpose(1, 0, 2, 3).astype(F32)

    sent, got = scatter_first(for_x, X)
    sent, got = scatter_second(for_x, got, X)
    mine = scatter_sum(for_x, got)
    theirs = shift(mine[1].astype(BF), ZL, 1)
    mine = (mine[0] + theirs.astype(F32)).astype(BF)
    mine = jnp.concatenate(from_zero([mine[k] for k in range(4)], y), 0)
    blocks = [mine[:, k * 320 : k * 320 + 320] for k in range(4)]
    return jnp.concatenate(from_zero(blocks, zh), 1)


def solution(mesh):
    fine = Mesh(mesh.devices.reshape(4, 4, 2, 4, 2), (Y, ZH, ZL, X, CORE))
    rows, cols = P((Y, ZH), TENSOR), P(TENSOR, (Y, ZH))
    in_specs = (cols, rows, rows, cols, rows, rows, cols, rows, rows, cols)
    return jax.shard_map(local, mesh=fine, in_specs=in_specs, out_specs=cols, check_vma=False)
```

```python
import jax
import jax.numpy as jnp
from jax import lax
from jax.experimental import pallas as pl
from jax.experimental.pallas import tpu as pltpu
from jax.sharding import Mesh, PartitionSpec as P

QB = 128
BF = jnp.bfloat16
F32 = jnp.float32
Y, ZH, ZL, X, CORE = "y", "zh", "zl", "x", "core"
TENSOR = (ZL, X, CORE)


def dot(a, b):
    return jnp.dot(a, b, preferred_element_type=F32)


def shift(value, axis, step):
    size = lax.axis_size(axis)
    return lax.ppermute(value, axis, [(i, (i + step) % size) for i in range(size)])


def after(value, *earlier):
    return lax.optimization_barrier((value, *earlier))[0]


def rows_kernel(me, scales, codes, *bases_and_out):
    *bases, out = bases_and_out
    first = (pl.program_id(0) + me[0]) % 4 * 10
    for i in range(10):
        for j in range(8):
            rows, cols = pl.ds(i * 32, 32), pl.ds(j * QB, QB)
            value = codes[rows, cols].astype(F32) * scales[(first + i) // 4, j]
            if bases:
                value += bases[i // 5][pl.ds(i % 5 * 32, 32), cols].astype(F32)
            out[rows, cols] = value.astype(BF)


def weight_rows(me, scales, codes, *bases):
    rows = pl.BlockSpec((320, 1024), lambda k, me: ((k + me[0]) % 4, 0))
    half = pl.BlockSpec((160, 1024), lambda k, me: ((k + me[0]) % 4, 0))
    return pl.pallas_call(
        rows_kernel,
        out_shape=jax.ShapeDtypeStruct((1280, 1024), BF),
        grid_spec=pltpu.PrefetchScalarGridSpec(
            num_scalar_prefetch=1,
            grid=(4,),
            in_specs=[pl.BlockSpec(memory_space=pltpu.SMEM), rows] + [half for _ in bases],
            out_specs=pl.BlockSpec((320, 1024), lambda k, me: (k, 0)),
        ),
        cost_estimate=pl.CostEstimate(flops=2621440, bytes_accessed=5242880, transcendentals=0),
        name="weight_rows",
    )(me, scales, codes, *bases)


def cols_kernel(me, scales, codes, out):
    j = pl.program_id(0)
    for i in range(8):
        rows = pl.ds(i * QB, QB)
        block = (codes[rows, :].astype(F32) * scales[i, j]).astype(BF).T
        for h in range(2):
            at = pl.multiple_of((2 * j + h + 20 - 5 * me[0]) % 20 * 64, 64)
            out[pl.ds(at, 64), rows] = block[h * 64 : h * 64 + 64]


def delta_cols(codes, scales, me):
    return pl.pallas_call(
        cols_kernel,
        out_shape=jax.ShapeDtypeStruct((1280, 1024), BF),
        grid_spec=pltpu.PrefetchScalarGridSpec(
            num_scalar_prefetch=1,
            grid=(10,),
            in_specs=[
                pl.BlockSpec(memory_space=pltpu.SMEM),
                pl.BlockSpec((1024, QB), lambda j, me: (0, j)),
            ],
            out_specs=pl.BlockSpec((1280, 1024), lambda j, me: (0, 0)),
        ),
        cost_estimate=pl.CostEstimate(flops=1310720, bytes_accessed=5242880, transcendentals=0),
        name="delta_cols",
    )(me, scales, codes)


def sum_kernel(delta, *pieces_and_out):
    at = 0
    *pieces, out = pieces_and_out
    for piece in pieces:
        for k in range(0, piece.shape[0], 32):
            value = delta[at : at + 32, :].astype(F32) + piece[k : k + 32, :].astype(F32)
            out[at : at + 32, :] = value.astype(BF)
            at += 32


def pieces_added(delta, *pieces):
    return pl.pallas_call(
        sum_kernel,
        out_shape=jax.ShapeDtypeStruct((1280, 1024), BF),
        in_specs=[pl.BlockSpec(memory_space=pltpu.VMEM)] * (1 + len(pieces)),
        out_specs=pl.BlockSpec(memory_space=pltpu.VMEM),
        compiler_params=pltpu.CompilerParams(vmem_limit_bytes=24 * 2**20),
        cost_estimate=pl.CostEstimate(flops=1310720, bytes_accessed=7864320, transcendentals=0),
        name="pieces_added",
    )(delta, *pieces)


def near(value, axis):
    return shift(value, axis, -1), shift(value, axis, 1)


def far(ahead, behind, axis):
    half = ahead.shape[0] // 2
    return shift(behind[:half], axis, 1), shift(ahead[half:], axis, -1)


def scatter_first(part, axis):
    opposite = part(2).astype(BF)
    half = opposite.shape[0] // 2
    sent = lax.optimization_barrier((opposite[:half], opposite[half:]))
    return sent, (shift(sent[0], axis, 1), shift(sent[1], axis, -1))


def scatter_second(part, got, axis):
    half = got[0].shape[0]
    ahead, behind = part(1), part(3)
    ahead = jnp.concatenate((ahead[:half] + got[0].astype(F32), ahead[half:]), 0).astype(BF)
    behind = jnp.concatenate((behind[:half], behind[half:] + got[1].astype(F32)), 0).astype(BF)
    return (ahead, behind), (shift(ahead, axis, 1), shift(behind, axis, -1))


def scatter_sum(part, got):
    return part(0) + got[0].astype(F32) + got[1].astype(F32)


def from_zero(pieces, me):
    return [lax.select_n((me * 3 + k) % 4, *pieces) for k in range(4)]


def local(
    normed,
    base_gate,
    base_up,
    base_down,
    codes_gate,
    codes_up,
    codes_down,
    scale_gate,
    scale_up,
    scale_down,
):
    y, zh = lax.axis_index(Y), lax.axis_index(ZH)

    me = zh.reshape(1).astype(jnp.int32)

    own = normed.reshape(4, 1, 16, 320)
    ahead, behind = near(own, ZH)
    opposite = shift(own, ZH, 2)
    gate_first = lax.all_gather(base_gate[:160], ZH, axis=0, tiled=True)
    feats = jnp.concatenate((own, ahead, opposite, behind), 3)
    feats = jnp.concatenate((feats, shift(feats, ZL, 1)), 1)
    ahead, behind = near(feats, X)
    first = shift(behind[:, :1], X, 1)
    second = shift(ahead[:, 1:], X, -1)
    first, second, gate_first = lax.optimization_barrier((first, second, gate_first))
    gate_second = lax.all_gather(after(base_gate, gate_first)[160:], ZH, axis=0, tiled=True)
    feats = jnp.concatenate((feats, ahead, first, second, behind), 1)
    feats = jnp.concatenate((feats, shift(feats, CORE, 1)), 1)
    feats = lax.optimization_barrier(feats.reshape(1024, 1280))

    def product(values, weight):
        def part(step):
            return dot(lax.dynamic_slice_in_dim(values, (y + step) % 4 * 256, 256, 0), weight)

        return part

    base_term = product(feats[:, :320], base_up)
    base_sent, base_got = scatter_first(base_term, Y)
    feats, codes_up = after((feats, codes_up), base_sent)
    base_term = product(feats[:, :320], base_up)
    delta_up = weight_rows(me, scale_up, codes_up)
    up_term = product(feats, delta_up)
    up_sent, up_got = scatter_first(up_term, Y)
    feats = after(feats, up_sent)
    up_term = product(feats, delta_up)

    base_got = after(base_got, up_sent)
    base_sent, base_got = scatter_second(base_term, base_got, Y)
    up_got = after(up_got, base_sent)
    up_sent, up_got = scatter_second(up_term, up_got, Y)

    gate_second = after(gate_second, up_sent)
    base_got = after(base_got, gate_second)
    base_part = lax.optimization_barrier(scatter_sum(base_term, base_got).astype(BF))
    total_first = lax.psum(base_part[:128], ZH)
    down_own = after(base_down.T, base_part)
    early_ahead, early_behind = near(down_own[:160], ZH)

    w_gate = weight_rows(me, scale_gate, after(codes_gate, base_part), gate_first, gate_second)
    up_got = after(up_got, w_gate)
    up = lax.optimization_barrier(scatter_sum(up_term, up_got))
    feats, total_first = lax.optimization_barrier((feats, total_first, up))[:2]
    total_second = lax.psum(after(base_part, total_first)[128:], ZH)
    gate_term = product(feats, w_gate)
    gate_sent, gate_got = scatter_first(gate_term, Y)
    gate_term = product(after(feats, gate_sent), w_gate)
    codes_down = after(codes_down, gate_sent)
    delta_down = delta_cols(codes_down, scale_down, me)

    early_ahead, early_behind = after((early_ahead, early_behind), gate_sent, delta_down)
    late_ahead, late_behind = near(after(down_own, early_ahead, early_behind)[160:], ZH)
    gate_got = after(gate_got, early_ahead, early_behind)
    gate_sent, gate_got = scatter_second(gate_term, gate_got, Y)

    total_second = after(total_second, *gate_sent)
    total = jnp.concatenate((total_first, total_second), 0)
    up = lax.optimization_barrier(up + total.astype(F32))
    late_ahead, late_behind = after((late_ahead, late_behind), up)
    far_early = shift(early_behind, ZH, 1)
    far_late = shift(late_ahead, ZH, -1)
    gate_got = after(gate_got, late_ahead, late_behind)
    gate = scatter_sum(gate_term, gate_got)
    hidden = (jax.nn.silu(gate) * up).astype(BF)
    ahead, behind = near(hidden, Y)
    opposite = far(ahead, behind, Y)

    far_early, far_late = after((far_early, far_late), ahead, behind)
    w_down = pieces_added(
        delta_down, down_own[:160], down_own[160:], early_ahead, late_ahead, far_early, far_late, early_behind, late_behind
    )
    opposite = after(opposite, w_down)
    pieces = (hidden, ahead, jnp.concatenate(opposite, 0), behind)

    def down(half):
        rows = jnp.concatenate([p[half * 128 : half * 128 + 128] for p in pieces], 0)
        return lax.dot_general(rows, w_down, (((1,), (1,)), ((), ())), preferred_element_type=F32)

    other = shift(down(1).astype(BF), CORE, 1)
    whole = lax.optimization_barrier((down(0) + other.astype(F32)).astype(BF))
    whole = whole.reshape(4, 4, 2, 16, 1280)

    def for_x(step):
        return whole[:, step].transpose(1, 0, 2, 3).astype(F32)

    sent, got = scatter_first(for_x, X)
    sent, got = scatter_second(for_x, got, X)
    mine = scatter_sum(for_x, got)
    theirs = shift(mine[1].astype(BF), ZL, 1)
    mine = (mine[0] + theirs.astype(F32)).astype(BF)
    mine = jnp.concatenate(from_zero([mine[k] for k in range(4)], y), 0)
    blocks = [mine[:, k * 320 : k * 320 + 320] for k in range(4)]
    return jnp.concatenate(from_zero(blocks, zh), 1)


def solution(mesh):
    fine = Mesh(mesh.devices.reshape(4, 4, 2, 4, 2), (Y, ZH, ZL, X, CORE))
    rows, cols = P((Y, ZH), TENSOR), P(TENSOR, (Y, ZH))
    in_specs = (cols, rows, rows, cols, rows, rows, cols, rows, rows, cols)
    return jax.shard_map(local, mesh=fine, in_specs=in_specs, out_specs=cols, check_vma=False)
```

```python
import jax
import jax.numpy as jnp
from jax import lax
from jax.experimental import pallas as pl
from jax.experimental.pallas import tpu as pltpu
from jax.sharding import Mesh, PartitionSpec as P

QB = 128
BF = jnp.bfloat16
F32 = jnp.float32
Y, ZH, ZL, X, CORE = "y", "zh", "zl", "x", "core"
TENSOR = (ZL, X, CORE)


def dot(a, b):
    return jnp.dot(a, b, preferred_element_type=F32)


def shift(value, axis, step):
    size = lax.axis_size(axis)
    return lax.ppermute(value, axis, [(i, (i + step) % size) for i in range(size)])


def after(value, *earlier):
    return lax.optimization_barrier((value, *earlier))[0]


def rows_kernel(me, scale_gate, scale_up, gate, up, out):
    first = (pl.program_id(0) + me[0]) % 4 * 5
    for at, scales, codes in ((0, scale_gate, gate), (1024, scale_up, up)):
        for i in range(5):
            for j in range(8):
                rows = pl.ds(i * 64, 64)
                value = codes[rows, pl.ds(j * QB, QB)].astype(F32) * scales[(first + i) // 2, j]
                out[rows, pl.ds(at + j * QB, QB)] = value.astype(BF)


def delta_rows(me, scale_gate, scale_up, gate, up):
    rows = pl.BlockSpec((320, 1024), lambda k, me: ((k + me[0]) % 4, 0))
    scalars = pl.BlockSpec(memory_space=pltpu.SMEM)
    return pl.pallas_call(
        rows_kernel,
        out_shape=jax.ShapeDtypeStruct((1280, 2048), BF),
        grid_spec=pltpu.PrefetchScalarGridSpec(
            num_scalar_prefetch=1,
            grid=(4,),
            in_specs=[scalars, scalars, rows, rows],
            out_specs=pl.BlockSpec((320, 2048), lambda k, me: (k, 0)),
        ),
        cost_estimate=pl.CostEstimate(flops=2621440, bytes_accessed=10485760, transcendentals=0),
        name="delta_rows",
    )(me, scale_gate, scale_up, gate, up)


def cols_kernel(me, scales, codes, out):
    j = pl.program_id(0)
    for i in range(8):
        rows = pl.ds(i * QB, QB)
        block = (codes[rows, :].astype(F32) * scales[i, j]).astype(BF).T
        for h in range(2):
            at = pl.multiple_of((2 * j + h + 20 - 5 * me[0]) % 20 * 64, 64)
            out[pl.ds(at, 64), rows] = block[h * 64 : h * 64 + 64]


def delta_cols(codes, scales, me):
    return pl.pallas_call(
        cols_kernel,
        out_shape=jax.ShapeDtypeStruct((1280, 1024), BF),
        grid_spec=pltpu.PrefetchScalarGridSpec(
            num_scalar_prefetch=1,
            grid=(10,),
            in_specs=[
                pl.BlockSpec(memory_space=pltpu.SMEM),
                pl.BlockSpec((1024, QB), lambda j, me: (0, j)),
            ],
            out_specs=pl.BlockSpec((1280, 1024), lambda j, me: (0, 0)),
        ),
        cost_estimate=pl.CostEstimate(flops=1310720, bytes_accessed=5242880, transcendentals=0),
        name="delta_cols",
    )(me, scales, codes)


def sum_kernel(delta, *pieces_and_out):
    *pieces, out = pieces_and_out
    at = 0
    for piece in pieces:
        for k in range(0, piece.shape[0], 16):
            rows = pl.ds(at, 16)
            base = piece[pl.ds(k, 16), :]
            out[rows, :] = (delta[rows, :].astype(F32) + base.astype(F32)).astype(BF)
            at += 16


def base_added(delta, *pieces):
    whole = pl.BlockSpec(memory_space=pltpu.VMEM)
    return pl.pallas_call(
        sum_kernel,
        out_shape=jax.ShapeDtypeStruct((1280, 1024), BF),
        in_specs=[whole] * (1 + len(pieces)),
        out_specs=whole,
        compiler_params=pltpu.CompilerParams(vmem_limit_bytes=24 * 2**20),
        cost_estimate=pl.CostEstimate(flops=1310720, bytes_accessed=7864320, transcendentals=0),
        name="base_added",
    )(delta, *pieces)


def near(value, axis):
    return shift(value, axis, -1), shift(value, axis, 1)


def far(ahead, behind, axis):
    half = ahead.shape[0] // 2
    return shift(behind[:half], axis, 1), shift(ahead[half:], axis, -1)


def scatter_first(part, half, axis):
    sent = part(2, (0, half)).astype(BF), part(2, (half, half)).astype(BF)
    sent = lax.optimization_barrier(sent)
    return sent, (shift(sent[0], axis, 1), shift(sent[1], axis, -1))


def scatter_second(part, got, axis):
    half = got[0].shape[0]
    first, second = (got[0].astype(F32), got[1].astype(F32))
    rest = ((0, 0),) * (first.ndim - 1)
    ahead = part(1, (0, 2 * half)) + jnp.pad(first, ((0, half),) + rest)
    behind = part(3, (0, 2 * half)) + jnp.pad(second, ((half, 0),) + rest)
    sent = lax.optimization_barrier((ahead.astype(BF), behind.astype(BF)))
    return sent, (shift(sent[0], axis, 1), shift(sent[1], axis, -1))


def scatter_sum(part, got):
    whole = part(0, (0, got[0].shape[0]))
    return whole + got[0].astype(F32) + got[1].astype(F32)


def from_zero(pieces, me):
    return [lax.select_n((me * 3 + k) % 4, *pieces) for k in range(4)]


def local(
    normed,
    base_gate,
    base_up,
    base_down,
    codes_gate,
    codes_up,
    codes_down,
    scale_gate,
    scale_up,
    scale_down,
):
    y, zh = lax.axis_index(Y), lax.axis_index(ZH)

    me = zh.reshape(1).astype(jnp.int32)

    base = jnp.concatenate((base_gate, base_up), 1)
    base_near = near(base, Y)
    own = normed.reshape(4, 16, 320)

    def kept_by(step):
        return lax.dynamic_index_in_dim(own, (y + step) % 4, 0, keepdims=False)

    ahead, behind = shift(kept_by(3), Y, -1), shift(kept_by(1), Y, 1)
    mine = jnp.concatenate((kept_by(0), ahead, behind, shift(kept_by(2), Y, 2)), 1)
    own = after(own, mine)
    ahead, behind = near(own, ZH)
    feats = jnp.concatenate((own, ahead, shift(own, ZH, 2), behind), 2)
    feats = jnp.concatenate((feats, mine[None]), 0)[:, None]
    feats = jnp.concatenate((feats, shift(feats, ZL, 1)), 1)
    down_own = base_down.T
    codes_gate, codes_up = after((codes_gate, codes_up), feats)
    delta = delta_rows(me, scale_gate, scale_up, codes_gate, codes_up)
    ahead, behind = after(near(feats, X), delta)
    first, second = shift(behind[:, :1], X, 1), shift(ahead[:, 1:], X, -1)
    first, second, base_near = lax.optimization_barrier((first, second, base_near))
    base_far = far(*base_near, Y)
    early_near = near(after(down_own, first)[:160], ZH)
    feats = jnp.concatenate((feats, ahead, first, second, behind), 1)
    feats = jnp.concatenate((feats, shift(feats, CORE, 1)), 1)
    feats = lax.optimization_barrier(feats.reshape(1280, 1280))
    mine, feats = feats[1024:], feats[:1024]

    def delta_term(step, rows):
        at = (y + step) % 4 * 256 + rows[0]
        return dot(lax.dynamic_slice_in_dim(feats, at, rows[1], 0), delta)

    delta_sent, delta_got = scatter_first(delta_term, 128, Y)
    feats = after(feats, delta_sent)

    early_near = after(early_near, delta_sent)
    early_far = far(*early_near, ZH)
    base = lax.optimization_barrier(jnp.concatenate((base, *base_near), 0))
    base_part = lax.optimization_barrier(dot(mine[:, :960], base))
    base_far = after(base_far, base_part)
    base_part += dot(mine[:, 960:1120], base_far[0]) + dot(mine[:, 1120:], base_far[1])
    base_part = lax.optimization_barrier(base_part)

    def base_term(step, rows):
        at = (zh + step) % 4 * 64 + rows[0]
        return lax.dynamic_slice_in_dim(base_part, at, rows[1], 0)

    base_sent, base_got = scatter_first(base_term, 32, ZH)
    delta_got = after(delta_got, base_sent)
    delta_sent, delta_got = scatter_second(delta_term, delta_got, Y)
    base_got, early_far = after((base_got, early_far), delta_sent)
    base_sent, base_got = scatter_second(base_term, base_got, ZH)
    codes_down = after(codes_down, base_sent)
    delta_down = delta_cols(codes_down, scale_down, me)
    base_got = after(base_got, delta_down)
    total = scatter_sum(base_term, base_got).astype(BF)
    ahead, behind = near(total, ZH)
    delta_got = after(delta_got, total)
    delta_sum = lax.optimization_barrier(scatter_sum(delta_term, delta_got))
    ahead, behind = after((ahead, behind), delta_sum)
    opposite = jnp.concatenate(far(ahead, behind, ZH), 0)
    total = jnp.concatenate(from_zero((total, ahead, opposite, behind), zh), 0)
    total = delta_sum + total.astype(F32)

    hidden = (jax.nn.silu(total[:, :1024]) * total[:, 1024:]).astype(BF)
    ahead, behind = near(hidden, Y)
    late_ahead, late_behind = near(after(down_own, total)[160:], ZH)
    opposite = far(ahead, behind, Y)
    late_ahead, late_behind = after((late_ahead, late_behind), ahead, behind)
    late_far = far(late_ahead, late_behind, ZH)
    opposite = after(opposite, late_ahead)
    late_far = after(late_far, *opposite)
    early = (down_own[:160], early_near[0], early_far, early_near[1])
    late = (down_own[160:], late_ahead, late_far, late_behind)
    down_base = [piece for pair in zip(early, late) for piece in pair]
    down_base[4:6] = *early_far, *late_far
    w_down = base_added(delta_down, *down_base)
    pieces = (hidden, ahead, jnp.concatenate(opposite, 0), behind)

    def down(half):
        rows = jnp.concatenate([p[half * 128 : half * 128 + 128] for p in pieces], 0)
        return lax.dot_general(rows, w_down, (((1,), (1,)), ((), ())), preferred_element_type=F32)

    other = shift(down(1).astype(BF), CORE, 1)
    whole = lax.optimization_barrier((down(0) + other.astype(F32)).astype(BF))
    whole = whole.reshape(4, 4, 2, 16, 1280)

    def for_x(step, rows):
        piece = whole[:, step, rows[0] : rows[0] + rows[1]]
        return piece.transpose(1, 0, 2, 3).astype(F32)

    sent, got = scatter_first(for_x, 1, X)
    sent, got = scatter_second(for_x, got, X)
    mine = scatter_sum(for_x, got)
    theirs = shift(mine[1].astype(BF), ZL, 1)
    mine = (mine[0] + theirs.astype(F32)).astype(BF)
    mine = jnp.concatenate(from_zero([mine[k] for k in range(4)], y), 0)
    blocks = [mine[:, k * 320 : k * 320 + 320] for k in range(4)]
    return jnp.concatenate(from_zero(blocks, zh), 1)


def solution(mesh):
    fine = Mesh(mesh.devices.reshape(4, 4, 2, 4, 2), (Y, ZH, ZL, X, CORE))
    rows, cols = P((Y, ZH), TENSOR), P(TENSOR, (Y, ZH))
    in_specs = (cols, rows, rows, cols, rows, rows, cols, rows, rows, cols)
    return jax.shard_map(local, mesh=fine, in_specs=in_specs, out_specs=cols, check_vma=False)
```

```python
import jax
import jax.numpy as jnp
from jax import lax
from jax.experimental import pallas as pl
from jax.experimental.pallas import tpu as pltpu
from jax.sharding import Mesh, PartitionSpec as P

QB = 128
BF = jnp.bfloat16
F32 = jnp.float32
Y, ZH, ZL, X, CORE = "y", "zh", "zl", "x", "core"
TENSOR = (ZL, X, CORE)


def dot(a, b):
    return jnp.dot(a, b, preferred_element_type=F32)


def shift(value, axis, step):
    size = lax.axis_size(axis)
    return lax.ppermute(value, axis, [(i, (i + step) % size) for i in range(size)])


def after(value, *earlier):
    return lax.optimization_barrier((value, *earlier))[0]


def rows_kernel(me, scale_gate, scale_up, gate, up, out):
    first = (pl.program_id(0) + me[0]) % 4 * 5
    for at, scales, codes in ((0, scale_gate, gate), (1024, scale_up, up)):
        for i in range(5):
            for j in range(8):
                rows = pl.ds(i * 64, 64)
                value = codes[rows, pl.ds(j * QB, QB)].astype(F32) * scales[(first + i) // 2, j]
                out[rows, pl.ds(at + j * QB, QB)] = value.astype(BF)


def delta_rows(me, scale_gate, scale_up, gate, up):
    rows = pl.BlockSpec((320, 1024), lambda k, me: ((k + me[0]) % 4, 0))
    scalars = pl.BlockSpec(memory_space=pltpu.SMEM)
    return pl.pallas_call(
        rows_kernel,
        out_shape=jax.ShapeDtypeStruct((1280, 2048), BF),
        grid_spec=pltpu.PrefetchScalarGridSpec(
            num_scalar_prefetch=1,
            grid=(4,),
            in_specs=[scalars, scalars, rows, rows],
            out_specs=pl.BlockSpec((320, 2048), lambda k, me: (k, 0)),
        ),
        cost_estimate=pl.CostEstimate(flops=2621440, bytes_accessed=10485760, transcendentals=0),
        name="delta_rows",
    )(me, scale_gate, scale_up, gate, up)


def cols_kernel(me, scales, codes, base, out):
    j = pl.program_id(0)
    for i in range(8):
        rows = pl.ds(i * QB, QB)
        block = (codes[rows, :].astype(F32) * scales[i, j]).astype(BF).T
        block = (block.astype(F32) + base[:, rows].astype(F32)).astype(BF)
        for h in range(2):
            at = pl.multiple_of((2 * j + h + 20 - 5 * me[0]) % 20 * 64, 64)
            out[pl.ds(at, 64), rows] = block[h * 64 : h * 64 + 64]


def weight_cols(me, scales, codes, base):
    return pl.pallas_call(
        cols_kernel,
        out_shape=jax.ShapeDtypeStruct((1280, 1024), BF),
        grid_spec=pltpu.PrefetchScalarGridSpec(
            num_scalar_prefetch=1,
            grid=(10,),
            in_specs=[
                pl.BlockSpec(memory_space=pltpu.SMEM),
                pl.BlockSpec((1024, QB), lambda j, me: (0, j)),
                pl.BlockSpec((QB, 1024), lambda j, me: (j, 0)),
            ],
            out_specs=pl.BlockSpec((1280, 1024), lambda j, me: (0, 0)),
        ),
        cost_estimate=pl.CostEstimate(flops=2621440, bytes_accessed=7864320, transcendentals=0),
        name="weight_cols",
    )(me, scales, codes, base)


def near(value, axis):
    return shift(value, axis, -1), shift(value, axis, 1)


def far(ahead, behind, axis):
    half = ahead.shape[0] // 2
    return shift(behind[:half], axis, 1), shift(ahead[half:], axis, -1)


def scatter_first(part, half, axis):
    sent = part(2, (0, half)).astype(BF), part(2, (half, half)).astype(BF)
    sent = lax.optimization_barrier(sent)
    return sent, (shift(sent[0], axis, 1), shift(sent[1], axis, -1))


def scatter_second(part, got, axis):
    half = got[0].shape[0]
    first, second = (got[0].astype(F32), got[1].astype(F32))
    rest = ((0, 0),) * (first.ndim - 1)
    ahead = part(1, (0, 2 * half)) + jnp.pad(first, ((0, half),) + rest)
    behind = part(3, (0, 2 * half)) + jnp.pad(second, ((half, 0),) + rest)
    sent = lax.optimization_barrier((ahead.astype(BF), behind.astype(BF)))
    return sent, (shift(sent[0], axis, 1), shift(sent[1], axis, -1))


def scatter_sum(part, got):
    whole = part(0, (0, got[0].shape[0]))
    return whole + got[0].astype(F32) + got[1].astype(F32)


def from_zero(pieces, me):
    return [lax.select_n((me * 3 + k) % 4, *pieces) for k in range(4)]


def local(
    normed,
    base_gate,
    base_up,
    base_down,
    codes_gate,
    codes_up,
    codes_down,
    scale_gate,
    scale_up,
    scale_down,
):
    y, zh = lax.axis_index(Y), lax.axis_index(ZH)

    me = zh.reshape(1).astype(jnp.int32)

    base = jnp.concatenate((base_gate, base_up), 1)
    base_near = near(base, Y)
    own = normed.reshape(4, 16, 320)

    def kept_by(step):
        return lax.dynamic_index_in_dim(own, (y + step) % 4, 0, keepdims=False)

    ahead, behind = shift(kept_by(3), Y, -1), shift(kept_by(1), Y, 1)
    mine = jnp.concatenate((kept_by(0), ahead, behind, shift(kept_by(2), Y, 2)), 1)
    ahead, behind = near(own, ZH)
    feats = jnp.concatenate((own, ahead, shift(own, ZH, 2), behind), 2)
    feats = jnp.concatenate((feats, mine[None]), 0)[:, None]
    feats = jnp.concatenate((feats, shift(feats, ZL, 1)), 1)
    down_base = lax.all_gather(base_down.T, ZH, axis=0, tiled=True)
    codes_gate, codes_up = after((codes_gate, codes_up), feats)
    delta = delta_rows(me, scale_gate, scale_up, codes_gate, codes_up)
    ahead, behind = near(feats, X)
    ahead, behind, base_near = lax.optimization_barrier((ahead, behind, base_near, delta))[:3]
    base_far = far(*base_near, Y)
    first, second = shift(behind[:, :1], X, 1), shift(ahead[:, 1:], X, -1)
    feats = jnp.concatenate((feats, ahead, first, second, behind), 1)
    feats = jnp.concatenate((feats, shift(feats, CORE, 1)), 1)
    feats, down_base = lax.optimization_barrier((feats, down_base))
    feats = feats.reshape(1280, 1280)
    mine, feats = feats[1024:], feats[:1024]

    def delta_term(step, rows):
        at = (y + step) % 4 * 256 + rows[0]
        return dot(lax.dynamic_slice_in_dim(feats, at, rows[1], 0), delta)

    base = lax.optimization_barrier(jnp.concatenate((base, *base_near), 0))
    delta_sent, delta_got = scatter_first(delta_term, 128, Y)
    feats = after(feats, delta_sent)
    base_far = after(base_far, delta_sent)
    base_part = dot(mine[:, :960], base)
    base_part += dot(mine[:, 960:1120], base_far[0]) + dot(mine[:, 1120:], base_far[1])
    base_part = lax.optimization_barrier(base_part)

    def base_term(step, rows):
        at = (zh + step) % 4 * 64 + rows[0]
        return lax.dynamic_slice_in_dim(base_part, at, rows[1], 0)

    base_sent, base_got = scatter_first(base_term, 32, ZH)
    base_sent, base_got = scatter_second(base_term, base_got, ZH)
    delta_got = after(delta_got, base_sent)
    delta_sent, delta_got = scatter_second(delta_term, delta_got, Y)
    base_got = after(base_got, delta_sent)
    total = scatter_sum(base_term, base_got).astype(BF)
    ahead, behind = near(total, ZH)
    codes_down = after(codes_down, total)
    w_down = weight_cols(me, scale_down, codes_down, down_base)
    feats = after(feats, total)
    ahead, behind = after((ahead, behind), w_down)
    opposite = jnp.concatenate(far(ahead, behind, ZH), 0)
    delta_got = after(delta_got, ahead, behind)
    delta_sum = lax.optimization_barrier(scatter_sum(delta_term, delta_got))
    opposite = after(opposite, delta_sum)
    total = jnp.concatenate(from_zero((total, ahead, opposite, behind), zh), 0)
    total = delta_sum + total.astype(F32)

    hidden = (jax.nn.silu(total[:, :1024]) * total[:, 1024:]).astype(BF)
    ahead, behind = near(hidden, Y)
    opposite = after(far(ahead, behind, Y), w_down)
    pieces = (hidden, ahead, jnp.concatenate(opposite, 0), behind)

    def down(half):
        rows = jnp.concatenate([p[half * 128 : half * 128 + 128] for p in pieces], 0)
        return lax.dot_general(rows, w_down, (((1,), (1,)), ((), ())), preferred_element_type=F32)

    other = shift(down(1).astype(BF), CORE, 1)
    whole = lax.optimization_barrier((down(0) + other.astype(F32)).astype(BF))
    whole = whole.reshape(4, 4, 2, 16, 1280)

    def for_x(step, rows):
        piece = whole[:, step, rows[0] : rows[0] + rows[1]]
        return piece.transpose(1, 0, 2, 3).astype(F32)

    sent, got = scatter_first(for_x, 1, X)
    sent, got = scatter_second(for_x, got, X)
    mine = scatter_sum(for_x, got)
    theirs = shift(mine[1].astype(BF), ZL, 1)
    mine = (mine[0] + theirs.astype(F32)).astype(BF)
    mine = jnp.concatenate(from_zero([mine[k] for k in range(4)], y), 0)
    blocks = [mine[:, k * 320 : k * 320 + 320] for k in range(4)]
    return jnp.concatenate(from_zero(blocks, zh), 1)


def solution(mesh):
    fine = Mesh(mesh.devices.reshape(4, 4, 2, 4, 2), (Y, ZH, ZL, X, CORE))
    rows, cols = P((Y, ZH), TENSOR), P(TENSOR, (Y, ZH))
    in_specs = (cols, rows, rows, cols, rows, rows, cols, rows, rows, cols)
    return jax.shard_map(local, mesh=fine, in_specs=in_specs, out_specs=cols, check_vma=False)
```

```python
import jax
import jax.numpy as jnp
from jax import lax
from jax.experimental import pallas as pl
from jax.experimental.pallas import tpu as pltpu
from jax.sharding import Mesh, PartitionSpec as P

QB = 128
BF = jnp.bfloat16
F32 = jnp.float32
Y, ZH, ZL, X, CORE = "y", "zh", "zl", "x", "core"
TENSOR = (ZL, X, CORE)


def dot(a, b):
    return jnp.dot(a, b, preferred_element_type=F32)


def shift(value, axis, step):
    size = lax.axis_size(axis)
    return lax.ppermute(value, axis, [(i, (i + step) % size) for i in range(size)])


def after(value, *earlier):
    return lax.optimization_barrier((value, *earlier))[0]


def rows_kernel(me, scale_gate, scale_up, gate, up, out):
    first = (pl.program_id(0) + me[0]) % 4 * 5
    for at, scales, codes in ((0, scale_gate, gate), (1024, scale_up, up)):
        for i in range(5):
            for j in range(8):
                rows = pl.ds(i * 64, 64)
                value = codes[rows, pl.ds(j * QB, QB)].astype(F32) * scales[(first + i) // 2, j]
                out[rows, pl.ds(at + j * QB, QB)] = value.astype(BF)


def delta_rows(me, scale_gate, scale_up, gate, up):
    rows = pl.BlockSpec((320, 1024), lambda k, me: ((k + me[0]) % 4, 0))
    scalars = pl.BlockSpec(memory_space=pltpu.SMEM)
    return pl.pallas_call(
        rows_kernel,
        out_shape=jax.ShapeDtypeStruct((1280, 2048), BF),
        grid_spec=pltpu.PrefetchScalarGridSpec(
            num_scalar_prefetch=1,
            grid=(4,),
            in_specs=[scalars, scalars, rows, rows],
            out_specs=pl.BlockSpec((320, 2048), lambda k, me: (k, 0)),
        ),
        cost_estimate=pl.CostEstimate(flops=2621440, bytes_accessed=10485760, transcendentals=0),
        name="delta_rows",
    )(me, scale_gate, scale_up, gate, up)


def cols_kernel(me, scales, codes, out):
    j = pl.program_id(0)
    for i in range(8):
        rows = pl.ds(i * QB, QB)
        block = (codes[rows, :].astype(F32) * scales[i, j]).astype(BF).T
        for h in range(2):
            at = pl.multiple_of((2 * j + h + 20 - 5 * me[0]) % 20 * 64, 64)
            out[pl.ds(at, 64), rows] = block[h * 64 : h * 64 + 64]


def delta_cols(codes, scales, me):
    return pl.pallas_call(
        cols_kernel,
        out_shape=jax.ShapeDtypeStruct((1280, 1024), BF),
        grid_spec=pltpu.PrefetchScalarGridSpec(
            num_scalar_prefetch=1,
            grid=(10,),
            in_specs=[
                pl.BlockSpec(memory_space=pltpu.SMEM),
                pl.BlockSpec((1024, QB), lambda j, me: (0, j)),
            ],
            out_specs=pl.BlockSpec((1280, 1024), lambda j, me: (0, 0)),
        ),
        cost_estimate=pl.CostEstimate(flops=1310720, bytes_accessed=5242880, transcendentals=0),
        name="delta_cols",
    )(me, scales, codes)


def sum_kernel(delta, *pieces_and_out):
    *pieces, out = pieces_and_out
    at = 0
    for piece in pieces:
        for k in range(0, piece.shape[0], 32):
            rows = pl.ds(at, 32)
            base = piece[pl.ds(k, 32), :]
            out[rows, :] = (delta[rows, :].astype(F32) + base.astype(F32)).astype(BF)
            at += 32


def base_added(delta, *pieces):
    whole = pl.BlockSpec(memory_space=pltpu.VMEM)
    return pl.pallas_call(
        sum_kernel,
        out_shape=jax.ShapeDtypeStruct(delta.shape, BF),
        in_specs=[whole] * (1 + len(pieces)),
        out_specs=whole,
        compiler_params=pltpu.CompilerParams(vmem_limit_bytes=24 * 2**20),
        cost_estimate=pl.CostEstimate(flops=1310720, bytes_accessed=7864320, transcendentals=0),
        name="base_added",
    )(delta, *pieces)


def near(value, axis):
    return shift(value, axis, -1), shift(value, axis, 1)


def far(ahead, behind, axis):
    half = ahead.shape[0] // 2
    return shift(behind[:half], axis, 1), shift(ahead[half:], axis, -1)


def scatter_first(part, half, axis):
    sent = part(2, (0, half)).astype(BF), part(2, (half, half)).astype(BF)
    sent = lax.optimization_barrier(sent)
    return sent, (shift(sent[0], axis, 1), shift(sent[1], axis, -1))


def scatter_second(part, got, axis):
    half = got[0].shape[0]
    first, second = (got[0].astype(F32), got[1].astype(F32))
    rest = ((0, 0),) * (first.ndim - 1)
    ahead = part(1, (0, 2 * half)) + jnp.pad(first, ((0, half),) + rest)
    behind = part(3, (0, 2 * half)) + jnp.pad(second, ((half, 0),) + rest)
    sent = lax.optimization_barrier((ahead.astype(BF), behind.astype(BF)))
    return sent, (shift(sent[0], axis, 1), shift(sent[1], axis, -1))


def scatter_sum(part, got):
    whole = part(0, (0, got[0].shape[0]))
    return whole + got[0].astype(F32) + got[1].astype(F32)


def from_zero(pieces, me):
    return [lax.select_n((me * 3 + k) % 4, *pieces) for k in range(4)]


def local(
    normed,
    base_gate,
    base_up,
    base_down,
    codes_gate,
    codes_up,
    codes_down,
    scale_gate,
    scale_up,
    scale_down,
):
    y, zh = lax.axis_index(Y), lax.axis_index(ZH)

    me = zh.reshape(1).astype(jnp.int32)

    own = normed.reshape(4, 16, 320)

    def kept_by(step):
        return lax.dynamic_index_in_dim(own, (y + step) % 4, 0, keepdims=False)

    ahead, behind = shift(kept_by(3), Y, -1), shift(kept_by(1), Y, 1)
    mine = jnp.concatenate((kept_by(0), ahead, behind, shift(kept_by(2), Y, 2)), 1)
    base = after(jnp.concatenate((base_gate, base_up), 1), mine)
    base_near = near(base, Y)
    ahead, behind = near(own, ZH)
    feats = jnp.concatenate((own, ahead, shift(own, ZH, 2), behind), 2)
    feats = jnp.concatenate((feats, mine[None]), 0)[:, None]
    feats = jnp.concatenate((feats, shift(feats, ZL, 1)), 1)
    codes_gate, codes_up = after((codes_gate, codes_up), feats)
    delta = delta_rows(me, scale_gate, scale_up, codes_gate, codes_up)
    ahead, behind = near(feats, X)
    ahead, behind = after((ahead, behind), delta)
    first, second = shift(behind[:, :1], X, 1), shift(ahead[:, 1:], X, -1)
    first, second, base_near = lax.optimization_barrier((first, second, base_near))
    base_far = far(*base_near, Y)
    down_own = after(base_down.T, first)
    down_near = near(down_own, ZH)
    feats = jnp.concatenate((feats, ahead, first, second, behind), 1)
    feats = jnp.concatenate((feats, shift(feats, CORE, 1)), 1)
    feats = lax.optimization_barrier(feats.reshape(1280, 1280))
    mine, feats = feats[1024:], feats[:1024]

    def delta_term(step, rows):
        at = (y + step) % 4 * 256 + rows[0]
        return dot(lax.dynamic_slice_in_dim(feats, at, rows[1], 0), delta)

    base = lax.optimization_barrier(jnp.concatenate((base, *base_near), 0))
    base_part = lax.optimization_barrier(dot(mine[:, :960], base))
    base_far = after(base_far, base_part)
    base_part += dot(mine[:, 960:1120], base_far[0]) + dot(mine[:, 1120:], base_far[1])
    base_part = lax.optimization_barrier(base_part)

    def base_term(step, rows):
        at = (zh + step) % 4 * 64 + rows[0]
        return lax.dynamic_slice_in_dim(base_part, at, rows[1], 0)

    base_sent, base_got = scatter_first(base_term, 32, ZH)
    feats = after(feats, base_sent)
    delta_sent, delta_got = scatter_first(delta_term, 128, Y)
    feats, base_got, down_near = after((feats, base_got, down_near), delta_sent)
    base_sent, base_got = scatter_second(base_term, base_got, ZH)
    delta_got = after(delta_got, base_sent, *down_near)
    delta_sent, delta_got = scatter_second(delta_term, delta_got, Y)
    base_got = after(base_got, delta_sent)
    total = scatter_sum(base_term, base_got).astype(BF)
    ahead, behind = near(total, ZH)
    feats, codes_down = after((feats, codes_down), total)
    delta_down = delta_cols(codes_down, scale_down, me)
    delta_own = lax.optimization_barrier(delta_term(0, (0, 256)))
    ahead, behind = after((ahead, behind), delta_down, delta_own)
    opposite = far(ahead, behind, ZH)
    delta_got, down_near = after((delta_got, down_near), ahead, behind)
    down_far = far(*down_near, ZH)
    opposite = jnp.concatenate(after(opposite, *delta_got), 0)
    total = jnp.concatenate(from_zero((total, ahead, opposite, behind), zh), 0).astype(F32)
    total += delta_own + delta_got[0].astype(F32) + delta_got[1].astype(F32)

    hidden = (jax.nn.silu(total[:, :1024]) * total[:, 1024:]).astype(BF)
    ahead, behind = near(hidden, Y)
    opposite = far(ahead, behind, Y)
    down_far = after(down_far, ahead, behind)
    w_down = base_added(delta_down, down_own, down_near[0], *down_far, down_near[1])
    opposite = after(opposite, w_down)
    pieces = (hidden, ahead, jnp.concatenate(opposite, 0), behind)

    def down(half):
        rows = jnp.concatenate([p[half * 128 : half * 128 + 128] for p in pieces], 0)
        return dot(rows, w_down.T)

    other = shift(down(1).astype(BF), CORE, 1)
    whole = lax.optimization_barrier((down(0) + other.astype(F32)).astype(BF))
    whole = whole.reshape(4, 4, 2, 16, 1280)

    def for_x(step, rows):
        piece = whole[:, step, rows[0] : rows[0] + rows[1]]
        return piece.transpose(1, 0, 2, 3).astype(F32)

    sent, got = scatter_first(for_x, 1, X)
    sent, got = scatter_second(for_x, got, X)
    mine = scatter_sum(for_x, got)
    theirs = shift(mine[1].astype(BF), ZL, 1)
    mine = (mine[0] + theirs.astype(F32)).astype(BF)
    mine = jnp.concatenate(from_zero([mine[k] for k in range(4)], y), 0)
    blocks = [mine[:, k * 320 : k * 320 + 320] for k in range(4)]
    return jnp.concatenate(from_zero(blocks, zh), 1)


def solution(mesh):
    fine = Mesh(mesh.devices.reshape(4, 4, 2, 4, 2), (Y, ZH, ZL, X, CORE))
    rows, cols = P((Y, ZH), TENSOR), P(TENSOR, (Y, ZH))
    in_specs = (cols, rows, rows, cols, rows, rows, cols, rows, rows, cols)
    return jax.shard_map(local, mesh=fine, in_specs=in_specs, out_specs=cols, check_vma=False)
```

```python
import jax
import jax.numpy as jnp
from jax import lax
from jax.experimental import pallas as pl
from jax.experimental.pallas import tpu as pltpu
from jax.sharding import Mesh, PartitionSpec as P

QB = 128
BF = jnp.bfloat16
F32 = jnp.float32
Y, ZH, ZL, X, CORE = "y", "zh", "zl", "x", "core"
TENSOR = (ZL, X, CORE)


def dot(a, b):
    return jnp.dot(a, b, preferred_element_type=F32)


def shift(value, axis, step):
    size = lax.axis_size(axis)
    return lax.ppermute(value, axis, [(i, (i + step) % size) for i in range(size)])


def after(value, *earlier):
    return lax.optimization_barrier((value, *earlier))[0]


def rows_kernel(me, scale_gate, scale_up, gate, up, out):
    first = (pl.program_id(0) + me[0]) % 4 * 5
    for at, scales, codes in ((0, scale_gate, gate), (1024, scale_up, up)):
        for i in range(5):
            for j in range(8):
                rows = pl.ds(i * 64, 64)
                value = codes[rows, pl.ds(j * QB, QB)].astype(F32) * scales[(first + i) // 2, j]
                out[rows, pl.ds(at + j * QB, QB)] = value.astype(BF)


def delta_rows(me, scale_gate, scale_up, gate, up):
    rows = pl.BlockSpec((320, 1024), lambda k, me: ((k + me[0]) % 4, 0))
    scalars = pl.BlockSpec(memory_space=pltpu.SMEM)
    return pl.pallas_call(
        rows_kernel,
        out_shape=jax.ShapeDtypeStruct((1280, 2048), BF),
        grid_spec=pltpu.PrefetchScalarGridSpec(
            num_scalar_prefetch=1,
            grid=(4,),
            in_specs=[scalars, scalars, rows, rows],
            out_specs=pl.BlockSpec((320, 2048), lambda k, me: (k, 0)),
        ),
        cost_estimate=pl.CostEstimate(flops=2621440, bytes_accessed=10485760, transcendentals=0),
        name="delta_rows",
    )(me, scale_gate, scale_up, gate, up)


def cols_kernel(me, scales, codes, out):
    j = pl.program_id(0)
    for i in range(8):
        rows = pl.ds(i * QB, QB)
        block = (codes[rows, :].astype(F32) * scales[i, j]).astype(BF).T
        for h in range(2):
            at = pl.multiple_of((2 * j + h + 20 - 5 * me[0]) % 20 * 64, 64)
            out[pl.ds(at, 64), rows] = block[h * 64 : h * 64 + 64]


def delta_cols(codes, scales, me):
    return pl.pallas_call(
        cols_kernel,
        out_shape=jax.ShapeDtypeStruct((1280, 1024), BF),
        grid_spec=pltpu.PrefetchScalarGridSpec(
            num_scalar_prefetch=1,
            grid=(10,),
            in_specs=[
                pl.BlockSpec(memory_space=pltpu.SMEM),
                pl.BlockSpec((1024, QB), lambda j, me: (0, j)),
            ],
            out_specs=pl.BlockSpec((1280, 1024), lambda j, me: (0, 0)),
        ),
        cost_estimate=pl.CostEstimate(flops=1310720, bytes_accessed=5242880, transcendentals=0),
        name="delta_cols",
    )(me, scales, codes)


def sum_kernel(delta, *pieces_and_out):
    *pieces, out = pieces_and_out
    at = 0
    for piece in pieces:
        for k in range(0, piece.shape[0], 32):
            rows = pl.ds(at, 32)
            base = piece[pl.ds(k, 32), :]
            out[rows, :] = (delta[rows, :].astype(F32) + base.astype(F32)).astype(BF)
            at += 32


def base_added(delta, *pieces):
    whole = pl.BlockSpec(memory_space=pltpu.VMEM)
    return pl.pallas_call(
        sum_kernel,
        out_shape=jax.ShapeDtypeStruct(delta.shape, BF),
        in_specs=[whole] * (1 + len(pieces)),
        out_specs=whole,
        compiler_params=pltpu.CompilerParams(vmem_limit_bytes=24 * 2**20),
        cost_estimate=pl.CostEstimate(flops=1310720, bytes_accessed=7864320, transcendentals=0),
        name="base_added",
    )(delta, *pieces)


def near(value, axis):
    return shift(value, axis, -1), shift(value, axis, 1)


def far(ahead, behind, axis):
    half = ahead.shape[0] // 2
    return shift(behind[:half], axis, 1), shift(ahead[half:], axis, -1)


def scatter_first(part, half, axis):
    sent = part(2, (0, half)).astype(BF), part(2, (half, half)).astype(BF)
    sent = lax.optimization_barrier(sent)
    return sent, (shift(sent[0], axis, 1), shift(sent[1], axis, -1))


def scatter_second(part, got, axis):
    half = got[0].shape[0]
    first, second = (got[0].astype(F32), got[1].astype(F32))
    rest = ((0, 0),) * (first.ndim - 1)
    ahead = part(1, (0, 2 * half)) + jnp.pad(first, ((0, half),) + rest)
    behind = part(3, (0, 2 * half)) + jnp.pad(second, ((half, 0),) + rest)
    sent = lax.optimization_barrier((ahead.astype(BF), behind.astype(BF)))
    return sent, (shift(sent[0], axis, 1), shift(sent[1], axis, -1))


def scatter_sum(part, got):
    whole = part(0, (0, got[0].shape[0]))
    return whole + got[0].astype(F32) + got[1].astype(F32)


def from_zero(pieces, me):
    return [lax.select_n((me * 3 + k) % 4, *pieces) for k in range(4)]


def local(
    normed,
    base_gate,
    base_up,
    base_down,
    codes_gate,
    codes_up,
    codes_down,
    scale_gate,
    scale_up,
    scale_down,
):
    y, zh = lax.axis_index(Y), lax.axis_index(ZH)

    me = zh.reshape(1).astype(jnp.int32)

    own = normed.reshape(4, 16, 320)

    def kept_by(step):
        return lax.dynamic_index_in_dim(own, (y + step) % 4, 0, keepdims=False)

    ahead, behind = shift(kept_by(3), Y, -1), shift(kept_by(1), Y, 1)
    mine = jnp.concatenate((kept_by(0), ahead, behind, shift(kept_by(2), Y, 2)), 1)
    base = after(jnp.concatenate((base_gate, base_up), 1), mine)
    base_near = near(base, Y)
    ahead, behind = near(own, ZH)
    feats = jnp.concatenate((own, ahead, shift(own, ZH, 2), behind), 2)
    feats = jnp.concatenate((feats, mine[None]), 0)[:, None]
    feats = jnp.concatenate((feats, shift(feats, ZL, 1)), 1)
    codes_gate, codes_up = after((codes_gate, codes_up), feats)
    delta = delta_rows(me, scale_gate, scale_up, codes_gate, codes_up)
    ahead, behind = near(feats, X)
    ahead, behind = after((ahead, behind), delta)
    first, second = shift(behind[:, :1], X, 1), shift(ahead[:, 1:], X, -1)
    first, second, base_near = lax.optimization_barrier((first, second, base_near))
    base_sent = lax.optimization_barrier((base_near[1][:160], base_near[0][160:]))
    base_far = shift(base_sent[0], Y, 1), shift(base_sent[1], Y, -1)
    down_own = after(base_down.T, first)
    down_near = near(down_own, ZH)
    first, second = after((first, second), *base_sent)
    feats = jnp.concatenate((feats, ahead, first, second, behind), 1)
    feats = jnp.concatenate((feats, shift(feats, CORE, 1)), 1)
    feats, base_near = lax.optimization_barrier((feats.reshape(1280, 1280), base_near))
    mine, feats = feats[1024:], feats[:1024]

    def delta_term(step, rows):
        at = (y + step) % 4 * 256 + rows[0]
        return dot(lax.dynamic_slice_in_dim(feats, at, rows[1], 0), delta)

    base = lax.optimization_barrier(jnp.concatenate((base, *base_near), 0))
    base_part = lax.optimization_barrier(dot(mine[:, :960], base))
    base_far = after(base_far, base_part)
    base_part += dot(mine[:, 960:1120], base_far[0]) + dot(mine[:, 1120:], base_far[1])
    base_part = lax.optimization_barrier(base_part)

    def base_term(step, rows):
        at = (zh + step) % 4 * 64 + rows[0]
        return lax.dynamic_slice_in_dim(base_part, at, rows[1], 0)

    base_sent, base_got = scatter_first(base_term, 32, ZH)
    feats = after(feats, base_sent)
    delta_sent, delta_got = scatter_first(delta_term, 128, Y)
    feats, base_got, down_near = after((feats, base_got, down_near), delta_sent)
    base_sent, base_got = scatter_second(base_term, base_got, ZH)
    ready = lax.optimization_barrier([delta_term(k, (0, 256)) for k in (1, 3)])
    delta_got = after(delta_got, base_sent, *down_near, *ready)
    delta_sent, delta_got = scatter_second(lambda k, rows: ready[k // 2], delta_got, Y)
    base_got = after(base_got, delta_sent)
    total = scatter_sum(base_term, base_got).astype(BF)
    ahead, behind = near(total, ZH)
    feats, codes_down = after((feats, codes_down), total)
    delta_down = delta_cols(codes_down, scale_down, me)
    delta_own = lax.optimization_barrier(delta_term(0, (0, 256)))
    ahead, behind = after((ahead, behind), delta_down, delta_own)
    opposite = far(ahead, behind, ZH)
    delta_got, down_near = after((delta_got, down_near), ahead, behind)
    down_far = far(*down_near, ZH)
    opposite = jnp.concatenate(after(opposite, *delta_got), 0)
    total = jnp.concatenate(from_zero((total, ahead, opposite, behind), zh), 0).astype(F32)
    total += delta_own + delta_got[0].astype(F32) + delta_got[1].astype(F32)

    hidden = (jax.nn.silu(total[:, :1024]) * total[:, 1024:]).astype(BF)
    ahead, behind = near(hidden, Y)
    opposite = far(ahead, behind, Y)
    down_far = after(down_far, ahead, behind)
    w_down = base_added(delta_down, down_own, down_near[0], *down_far, down_near[1])
    opposite = after(opposite, w_down)
    pieces = (hidden, ahead, jnp.concatenate(opposite, 0), behind)

    def down(half):
        rows = jnp.concatenate([p[half * 128 : half * 128 + 128] for p in pieces], 0)
        return dot(rows, w_down.T)

    other = shift(down(1).astype(BF), CORE, 1)
    whole = lax.optimization_barrier((down(0) + other.astype(F32)).astype(BF))
    whole = whole.reshape(4, 4, 2, 16, 1280)

    def for_x(step, rows):
        piece = whole[:, step, rows[0] : rows[0] + rows[1]]
        return piece.transpose(1, 0, 2, 3).astype(F32)

    sent, got = scatter_first(for_x, 1, X)
    sent, got = scatter_second(for_x, got, X)
    mine = scatter_sum(for_x, got)
    theirs = shift(mine[1].astype(BF), ZL, 1)
    mine = (mine[0] + theirs.astype(F32)).astype(BF)
    mine = jnp.concatenate(from_zero([mine[k] for k in range(4)], y), 0)
    blocks = [mine[:, k * 320 : k * 320 + 320] for k in range(4)]
    return jnp.concatenate(from_zero(blocks, zh), 1)


def solution(mesh):
    fine = Mesh(mesh.devices.reshape(4, 4, 2, 4, 2), (Y, ZH, ZL, X, CORE))
    rows, cols = P((Y, ZH), TENSOR), P(TENSOR, (Y, ZH))
    in_specs = (cols, rows, rows, cols, rows, rows, cols, rows, rows, cols)
    return jax.shard_map(local, mesh=fine, in_specs=in_specs, out_specs=cols, check_vma=False)
```

```python
import jax
import jax.numpy as jnp
from jax import lax
from jax.experimental import pallas as pl
from jax.experimental.pallas import tpu as pltpu
from jax.sharding import Mesh, PartitionSpec as P

QB = 128
BF = jnp.bfloat16
F32 = jnp.float32
Y, ZH, ZL, X, CORE = "y", "zh", "zl", "x", "core"
TENSOR = (ZL, X, CORE)


def dot(a, b):
    return jnp.dot(a, b, preferred_element_type=F32)


def shift(value, axis, step):
    size = lax.axis_size(axis)
    return lax.ppermute(value, axis, [(i, (i + step) % size) for i in range(size)])


def after(value, *earlier):
    return lax.optimization_barrier((value, *earlier))[0]


def rows_kernel(me, scale_gate, scale_up, gate, up, out):
    first = (pl.program_id(0) + me[0]) % 4 * 5
    for at, scales, codes in ((0, scale_gate, gate), (1024, scale_up, up)):
        for i in range(5):
            for j in range(8):
                rows = pl.ds(i * 64, 64)
                value = codes[rows, pl.ds(j * QB, QB)].astype(F32) * scales[(first + i) // 2, j]
                out[rows, pl.ds(at + j * QB, QB)] = value.astype(BF)


def delta_rows(me, scale_gate, scale_up, gate, up):
    rows = pl.BlockSpec((320, 1024), lambda k, me: ((k + me[0]) % 4, 0))
    scalars = pl.BlockSpec(memory_space=pltpu.SMEM)
    return pl.pallas_call(
        rows_kernel,
        out_shape=jax.ShapeDtypeStruct((1280, 2048), BF),
        grid_spec=pltpu.PrefetchScalarGridSpec(
            num_scalar_prefetch=1,
            grid=(4,),
            in_specs=[scalars, scalars, rows, rows],
            out_specs=pl.BlockSpec((320, 2048), lambda k, me: (k, 0)),
        ),
        cost_estimate=pl.CostEstimate(flops=2621440, bytes_accessed=10485760, transcendentals=0),
        name="delta_rows",
    )(me, scale_gate, scale_up, gate, up)


def cols_kernel(me, scales, codes, out):
    j = pl.program_id(0)
    for i in range(8):
        rows = pl.ds(i * QB, QB)
        block = (codes[rows, :].astype(F32) * scales[i, j]).astype(BF).T
        for h in range(2):
            at = pl.multiple_of((2 * j + h + 20 - 5 * me[0]) % 20 * 64, 64)
            out[pl.ds(at, 64), rows] = block[h * 64 : h * 64 + 64]


def delta_cols(codes, scales, me):
    return pl.pallas_call(
        cols_kernel,
        out_shape=jax.ShapeDtypeStruct((1280, 1024), BF),
        grid_spec=pltpu.PrefetchScalarGridSpec(
            num_scalar_prefetch=1,
            grid=(10,),
            in_specs=[
                pl.BlockSpec(memory_space=pltpu.SMEM),
                pl.BlockSpec((1024, QB), lambda j, me: (0, j)),
            ],
            out_specs=pl.BlockSpec((1280, 1024), lambda j, me: (0, 0)),
        ),
        cost_estimate=pl.CostEstimate(flops=1310720, bytes_accessed=5242880, transcendentals=0),
        name="delta_cols",
    )(me, scales, codes)


def sum_kernel(delta, *pieces_and_out):
    *pieces, out = pieces_and_out
    at = 0
    for piece in pieces:
        for k in range(0, piece.shape[0], 32):
            rows = pl.ds(at, 32)
            base = piece[pl.ds(k, 32), :]
            out[rows, :] = (delta[rows, :].astype(F32) + base.astype(F32)).astype(BF)
            at += 32


def base_added(delta, *pieces):
    whole = pl.BlockSpec(memory_space=pltpu.VMEM)
    return pl.pallas_call(
        sum_kernel,
        out_shape=jax.ShapeDtypeStruct(delta.shape, BF),
        in_specs=[whole] * (1 + len(pieces)),
        out_specs=whole,
        compiler_params=pltpu.CompilerParams(vmem_limit_bytes=24 * 2**20),
        cost_estimate=pl.CostEstimate(flops=1310720, bytes_accessed=7864320, transcendentals=0),
        name="base_added",
    )(delta, *pieces)


def near(value, axis):
    return shift(value, axis, -1), shift(value, axis, 1)


def far(ahead, behind, axis):
    half = ahead.shape[0] // 2
    return shift(behind[:half], axis, 1), shift(ahead[half:], axis, -1)


def scatter_first(part, half, axis):
    sent = part(2, (0, half)).astype(BF), part(2, (half, half)).astype(BF)
    sent = lax.optimization_barrier(sent)
    return sent, (shift(sent[0], axis, 1), shift(sent[1], axis, -1))


def scatter_second(part, got, axis):
    half = got[0].shape[0]
    first, second = (got[0].astype(F32), got[1].astype(F32))
    rest = ((0, 0),) * (first.ndim - 1)
    ahead = part(1, (0, 2 * half)) + jnp.pad(first, ((0, half),) + rest)
    behind = part(3, (0, 2 * half)) + jnp.pad(second, ((half, 0),) + rest)
    sent = lax.optimization_barrier((ahead.astype(BF), behind.astype(BF)))
    return sent, (shift(sent[0], axis, 1), shift(sent[1], axis, -1))


def scatter_sum(part, got):
    whole = part(0, (0, got[0].shape[0]))
    return whole + got[0].astype(F32) + got[1].astype(F32)


def from_zero(pieces, me):
    return [lax.select_n((me * 3 + k) % 4, *pieces) for k in range(4)]


def local(
    normed,
    base_gate,
    base_up,
    base_down,
    codes_gate,
    codes_up,
    codes_down,
    scale_gate,
    scale_up,
    scale_down,
):
    y, zh = lax.axis_index(Y), lax.axis_index(ZH)

    me = zh.reshape(1).astype(jnp.int32)

    own = normed.reshape(4, 16, 320)

    def kept_by(step):
        return lax.dynamic_index_in_dim(own, (y + step) % 4, 0, keepdims=False)

    ahead, behind = shift(kept_by(3), Y, -1), shift(kept_by(1), Y, 1)
    mine = jnp.concatenate((kept_by(0), ahead, behind, shift(kept_by(2), Y, 2)), 1)
    base = after(jnp.concatenate((base_gate, base_up), 1), mine)
    base_near = near(base, Y)
    ahead, behind = near(own, ZH)
    feats = jnp.concatenate((own, ahead, shift(own, ZH, 2), behind), 2)
    feats = jnp.concatenate((feats, mine[None]), 0)[:, None]
    feats = jnp.concatenate((feats, shift(feats, ZL, 1)), 1)
    codes_gate, codes_up = after((codes_gate, codes_up), feats)
    delta = delta_rows(me, scale_gate, scale_up, codes_gate, codes_up)
    ahead, behind = near(feats, X)
    ahead, behind = after((ahead, behind), delta)
    first, second = shift(behind[:, :1], X, 1), shift(ahead[:, 1:], X, -1)
    first, second, base_near = lax.optimization_barrier((first, second, base_near))
    base_sent = lax.optimization_barrier((base_near[1][:160], base_near[0][160:]))
    base_far = shift(base_sent[0], Y, 1), shift(base_sent[1], Y, -1)
    down_own = after(base_down.T, first)
    down_near = near(down_own, ZH)
    first, second = after((first, second), *base_sent)
    feats = jnp.concatenate((feats, ahead, first, second, behind), 1)
    feats = jnp.concatenate((feats, shift(feats, CORE, 1)), 1)
    feats, base_near = lax.optimization_barrier((feats.reshape(1280, 1280), base_near))
    mine, feats = feats[1024:], feats[:1024]

    def delta_term(step, rows):
        at = (y + step) % 4 * 256 + rows[0]
        return dot(lax.dynamic_slice_in_dim(feats, at, rows[1], 0), delta)

    base = lax.optimization_barrier(jnp.concatenate((base, *base_near), 0))
    base_part = lax.optimization_barrier(dot(mine[:, :960], base))
    base_far = after(base_far, base_part)
    base_part += dot(mine[:, 960:1120], base_far[0]) + dot(mine[:, 1120:], base_far[1])
    base_part = lax.optimization_barrier(base_part)

    def base_term(step, rows):
        at = (zh + step) % 4 * 64 + rows[0]
        return lax.dynamic_slice_in_dim(base_part, at, rows[1], 0)

    base_sent, base_got = scatter_first(base_term, 32, ZH)
    feats = after(feats, base_sent)
    delta_sent, delta_got = scatter_first(delta_term, 128, Y)
    feats, base_got, down_near = after((feats, base_got, down_near), delta_sent)
    base_sent, base_got = scatter_second(base_term, base_got, ZH)
    ready = lax.optimization_barrier([delta_term(k, (0, 256)) for k in (1, 3)])
    delta_got = after(delta_got, base_sent, *down_near, *ready)
    delta_sent, delta_got = scatter_second(lambda k, rows: ready[k // 2], delta_got, Y)
    base_got = after(base_got, delta_sent)
    total = scatter_sum(base_term, base_got).astype(BF)
    ahead, behind = near(total, ZH)
    feats, codes_down = after((feats, codes_down), total)
    delta_down = delta_cols(codes_down, scale_down, me)
    delta_own = lax.optimization_barrier(delta_term(0, (0, 256)))
    ahead, behind = after((ahead, behind), delta_down, delta_own)
    opposite = far(ahead, behind, ZH)
    delta_got, down_near = after((delta_got, down_near), ahead, behind)
    down_far = far(*down_near, ZH)
    opposite = after(opposite, *delta_got)
    opposite = jnp.pad(opposite[0], ((0, 32), (0, 0))) + jnp.pad(opposite[1], ((32, 0), (0, 0)))
    total = jnp.concatenate(from_zero((total, ahead, opposite, behind), zh), 0).astype(F32)
    total += delta_own + delta_got[0].astype(F32) + delta_got[1].astype(F32)

    hidden = (jax.nn.silu(total[:, :1024]) * total[:, 1024:]).astype(BF)
    ahead, behind = near(hidden, Y)
    opposite = far(ahead, behind, Y)
    down_far = after(down_far, ahead, behind)
    w_down = base_added(delta_down, down_own, down_near[0], *down_far, down_near[1])
    opposite = after(opposite, w_down)
    pieces = (hidden, ahead, jnp.concatenate(opposite, 0), behind)

    def down(half):
        rows = jnp.concatenate([p[half * 128 : half * 128 + 128] for p in pieces], 0)
        return dot(rows, w_down.T)

    sent = lax.optimization_barrier(down(1).astype(BF))
    other = shift(sent, CORE, 1)
    kept = lax.optimization_barrier(down(0))
    other = after(other, kept)
    whole = lax.optimization_barrier((kept + other.astype(F32)).astype(BF))
    whole = whole.reshape(4, 4, 2, 16, 1280)

    def for_x(step, rows):
        piece = whole[:, step, rows[0] : rows[0] + rows[1]]
        return piece.transpose(1, 0, 2, 3).astype(F32)

    sent, got = scatter_first(for_x, 1, X)
    sent, got = scatter_second(for_x, got, X)
    mine = scatter_sum(for_x, got)
    theirs = shift(mine[1].astype(BF), ZL, 1)
    mine = (mine[0] + theirs.astype(F32)).astype(BF)
    mine = jnp.concatenate(from_zero([mine[k] for k in range(4)], y), 0)
    blocks = [mine[:, k * 320 : k * 320 + 320] for k in range(4)]
    return jnp.concatenate(from_zero(blocks, zh), 1)


def solution(mesh):
    fine = Mesh(mesh.devices.reshape(4, 4, 2, 4, 2), (Y, ZH, ZL, X, CORE))
    rows, cols = P((Y, ZH), TENSOR), P(TENSOR, (Y, ZH))
    in_specs = (cols, rows, rows, cols, rows, rows, cols, rows, rows, cols)
    return jax.shard_map(local, mesh=fine, in_specs=in_specs, out_specs=cols, check_vma=False)
```

```python
import jax
import jax.numpy as jnp
from jax import lax
from jax.experimental import pallas as pl
from jax.experimental.pallas import tpu as pltpu
from jax.sharding import Mesh, PartitionSpec as P

QB = 128
BF = jnp.bfloat16
F32 = jnp.float32
Y, ZH, ZL, X, CORE = "y", "zh", "zl", "x", "core"
TENSOR = (ZL, X, CORE)


def dot(a, b):
    return jnp.dot(a, b, preferred_element_type=F32)


def shift(value, axis, step):
    size = lax.axis_size(axis)
    return lax.ppermute(value, axis, [(i, (i + step) % size) for i in range(size)])


def after(value, *earlier):
    return lax.optimization_barrier((value, *earlier))[0]


def rows_kernel(me, scale_gate, scale_up, gate, up, out):
    first = (pl.program_id(0) + me[0]) % 4 * 5
    for at, scales, codes in ((0, scale_gate, gate), (1024, scale_up, up)):
        for i in range(5):
            for j in range(8):
                rows = pl.ds(i * 64, 64)
                value = codes[rows, pl.ds(j * QB, QB)].astype(F32) * scales[(first + i) // 2, j]
                out[rows, pl.ds(at + j * QB, QB)] = value.astype(BF)


def delta_rows(me, scale_gate, scale_up, gate, up):
    rows = pl.BlockSpec((320, 1024), lambda k, me: ((k + me[0]) % 4, 0))
    scalars = pl.BlockSpec(memory_space=pltpu.SMEM)
    return pl.pallas_call(
        rows_kernel,
        out_shape=jax.ShapeDtypeStruct((1280, 2048), BF),
        grid_spec=pltpu.PrefetchScalarGridSpec(
            num_scalar_prefetch=1,
            grid=(4,),
            in_specs=[scalars, scalars, rows, rows],
            out_specs=pl.BlockSpec((320, 2048), lambda k, me: (k, 0)),
        ),
        cost_estimate=pl.CostEstimate(flops=2621440, bytes_accessed=10485760, transcendentals=0),
        name="delta_rows",
    )(me, scale_gate, scale_up, gate, up)


def cols_kernel(scales, codes, out):
    j = pl.program_id(0)
    for i in range(8):
        rows = pl.ds(i * QB, QB)
        out[:, rows] = (codes[rows, :].astype(F32) * scales[i, j]).astype(BF).T


def delta_cols(codes, scales):
    return pl.pallas_call(
        cols_kernel,
        out_shape=jax.ShapeDtypeStruct((1280, 1024), BF),
        grid=(10,),
        in_specs=[
            pl.BlockSpec(memory_space=pltpu.SMEM),
            pl.BlockSpec((1024, QB), lambda j: (0, j)),
        ],
        out_specs=pl.BlockSpec((QB, 1024), lambda j: (j, 0)),
        cost_estimate=pl.CostEstimate(flops=1310720, bytes_accessed=5242880, transcendentals=0),
        name="delta_cols",
    )(scales, codes)


def sum_kernel(me, delta, *pieces_and_out):
    *pieces, out = pieces_and_out
    at = 0
    for piece in pieces:
        for k in range(0, piece.shape[0], 32):
            block = (me[0] + at // 320) % 4 * 320
            rows = pl.ds(pl.multiple_of(block + at % 320, 32), 32)
            base = piece[pl.ds(k, 32), :]
            out[rows, :] = (delta[rows, :].astype(F32) + base.astype(F32)).astype(BF)
            at += 32


def base_added(me, delta, *pieces):
    whole = pl.BlockSpec(memory_space=pltpu.VMEM)
    return pl.pallas_call(
        sum_kernel,
        out_shape=jax.ShapeDtypeStruct((1280, 1024), BF),
        in_specs=[pl.BlockSpec(memory_space=pltpu.SMEM)] + [whole] * (1 + len(pieces)),
        out_specs=whole,
        compiler_params=pltpu.CompilerParams(vmem_limit_bytes=24 * 2**20),
        cost_estimate=pl.CostEstimate(flops=1310720, bytes_accessed=7864320, transcendentals=0),
        name="base_added",
    )(me, delta, *pieces)


def near(value, axis):
    return shift(value, axis, -1), shift(value, axis, 1)


def far(ahead, behind, axis):
    half = ahead.shape[0] // 2
    return shift(behind[:half], axis, 1), shift(ahead[half:], axis, -1)


def scatter_first(part, half, axis):
    sent = part(2, (0, half)).astype(BF), part(2, (half, half)).astype(BF)
    sent = lax.optimization_barrier(sent)
    return sent, (shift(sent[0], axis, 1), shift(sent[1], axis, -1))


def scatter_second(part, got, axis):
    half = got[0].shape[0]
    first, second = (got[0].astype(F32), got[1].astype(F32))
    rest = ((0, 0),) * (first.ndim - 1)
    ahead = part(1, (0, 2 * half)) + jnp.pad(first, ((0, half),) + rest)
    behind = part(3, (0, 2 * half)) + jnp.pad(second, ((half, 0),) + rest)
    sent = lax.optimization_barrier((ahead.astype(BF), behind.astype(BF)))
    return sent, (shift(sent[0], axis, 1), shift(sent[1], axis, -1))


def scatter_sum(part, got):
    whole = part(0, (0, got[0].shape[0]))
    return whole + got[0].astype(F32) + got[1].astype(F32)


def from_zero(pieces, me):
    return [lax.select_n((me * 3 + k) % 4, *pieces) for k in range(4)]


def local(
    normed,
    base_gate,
    base_up,
    base_down,
    codes_gate,
    codes_up,
    codes_down,
    scale_gate,
    scale_up,
    scale_down,
):
    y, zh = lax.axis_index(Y), lax.axis_index(ZH)

    me = zh.reshape(1).astype(jnp.int32)

    own = normed.reshape(4, 16, 320)

    def kept_by(step):
        return lax.dynamic_index_in_dim(own, (y + step) % 4, 0, keepdims=False)

    ahead, behind = shift(kept_by(3), Y, -1), shift(kept_by(1), Y, 1)
    mine = jnp.concatenate((kept_by(0), ahead, behind, shift(kept_by(2), Y, 2)), 1)
    base = after(jnp.concatenate((base_gate, base_up), 1), mine)
    base_near = near(base, Y)
    ahead, behind = near(own, ZH)
    feats = jnp.concatenate((own, ahead, shift(own, ZH, 2), behind), 2)
    feats = jnp.concatenate((feats, mine[None]), 0)[:, None]
    feats = jnp.concatenate((feats, shift(feats, ZL, 1)), 1)
    codes_gate, codes_up = after((codes_gate, codes_up), feats)
    delta = delta_rows(me, scale_gate, scale_up, codes_gate, codes_up)
    ahead, behind = near(feats, X)
    ahead, behind = after((ahead, behind), delta)
    first, second = shift(behind[:, :1], X, 1), shift(ahead[:, 1:], X, -1)
    first, second, base_near = lax.optimization_barrier((first, second, base_near))
    base_sent = lax.optimization_barrier((base_near[1][:160], base_near[0][160:]))
    base_far = shift(base_sent[0], Y, 1), shift(base_sent[1], Y, -1)
    down_own = after(base_down.T, first)
    down_near = near(down_own, ZH)
    first, second = after((first, second), *base_sent)
    feats = jnp.concatenate((feats, ahead, first, second, behind), 1)
    feats = jnp.concatenate((feats, shift(feats, CORE, 1)), 1)
    feats, base_near = lax.optimization_barrier((feats.reshape(1280, 1280), base_near))
    mine, feats = feats[1024:], feats[:1024]

    def delta_term(step, rows):
        at = (y + step) % 4 * 256 + rows[0]
        return dot(lax.dynamic_slice_in_dim(feats, at, rows[1], 0), delta)

    base = lax.optimization_barrier(jnp.concatenate((base, *base_near), 0))
    base_part = lax.optimization_barrier(dot(mine[:, :960], base))
    base_far = after(base_far, base_part)
    base_part += dot(mine[:, 960:1120], base_far[0]) + dot(mine[:, 1120:], base_far[1])
    base_part = lax.optimization_barrier(base_part)

    def base_term(step, rows):
        at = (zh + step) % 4 * 64 + rows[0]
        return lax.dynamic_slice_in_dim(base_part, at, rows[1], 0)

    base_sent, base_got = scatter_first(base_term, 32, ZH)
    feats = after(feats, base_sent)
    delta_sent, delta_got = scatter_first(delta_term, 128, Y)
    feats, base_got, down_near = after((feats, base_got, down_near), delta_sent)
    base_sent, base_got = scatter_second(base_term, base_got, ZH)
    ready = lax.optimization_barrier([delta_term(k, (0, 256)) for k in (1, 3)])
    delta_got = after(delta_got, base_sent, *down_near, *ready)
    delta_sent, delta_got = scatter_second(lambda k, rows: ready[k // 2], delta_got, Y)
    base_got = after(base_got, delta_sent)
    total = scatter_sum(base_term, base_got).astype(BF)
    ahead, behind = near(total, ZH)
    feats, codes_down = after((feats, codes_down), total)
    delta_down = delta_cols(codes_down, scale_down)
    delta_own = lax.optimization_barrier(delta_term(0, (0, 256)))
    ahead, behind = after((ahead, behind), delta_down, delta_own)
    opposite = far(ahead, behind, ZH)
    delta_got, down_near = after((delta_got, down_near), ahead, behind)
    down_far = far(*down_near, ZH)
    opposite = after(opposite, *delta_got)
    opposite = jnp.pad(opposite[0], ((0, 32), (0, 0))) + jnp.pad(opposite[1], ((32, 0), (0, 0)))
    total = jnp.concatenate(from_zero((total, ahead, opposite, behind), zh), 0).astype(F32)
    total += delta_own + delta_got[0].astype(F32) + delta_got[1].astype(F32)

    hidden = (jax.nn.silu(total[:, :1024]) * total[:, 1024:]).astype(BF)
    ahead, behind = near(hidden, Y)
    opposite = far(ahead, behind, Y)
    down_far = after(down_far, ahead, behind)
    w_down = base_added(me, delta_down, down_own, down_near[0], *down_far, down_near[1])
    opposite = after(opposite, w_down)
    pieces = (hidden, ahead, jnp.concatenate(opposite, 0), behind)

    def down(half):
        rows = jnp.concatenate([p[half * 128 : half * 128 + 128] for p in pieces], 0)
        return dot(rows, w_down.T)

    sent = lax.optimization_barrier(down(1).astype(BF))
    other = shift(sent, CORE, 1)
    kept = lax.optimization_barrier(down(0))
    other = after(other, kept)
    whole = lax.optimization_barrier((kept + other.astype(F32)).astype(BF))
    whole = whole.reshape(4, 4, 2, 16, 1280)

    def for_x(step, rows):
        piece = whole[:, step, rows[0] : rows[0] + rows[1]]
        return piece.transpose(1, 0, 2, 3).astype(F32)

    sent, got = scatter_first(for_x, 1, X)
    sent, got = scatter_second(for_x, got, X)
    mine = scatter_sum(for_x, got)
    theirs = shift(mine[1].astype(BF), ZL, 1)
    mine = (mine[0] + theirs.astype(F32)).astype(BF)
    return jnp.concatenate(from_zero([mine[k] for k in range(4)], y), 0)


def solution(mesh):
    fine = Mesh(mesh.devices.reshape(4, 4, 2, 4, 2), (Y, ZH, ZL, X, CORE))
    rows, cols = P((Y, ZH), TENSOR), P(TENSOR, (Y, ZH))
    in_specs = (cols, rows, rows, cols, rows, rows, cols, rows, rows, cols)
    return jax.shard_map(local, mesh=fine, in_specs=in_specs, out_specs=cols, check_vma=False)
```

```python
import jax
import jax.numpy as jnp
from jax import lax
from jax.experimental import pallas as pl
from jax.experimental.pallas import tpu as pltpu
from jax.sharding import Mesh, PartitionSpec as P

QB = 128
BF = jnp.bfloat16
F32 = jnp.float32
Y, ZH, ZL, X, CORE = "y", "zh", "zl", "x", "core"
TENSOR = (ZL, X, CORE)


def dot(a, b):
    return jnp.dot(a, b, preferred_element_type=F32)


def shift(value, axis, step):
    size = lax.axis_size(axis)
    return lax.ppermute(value, axis, [(i, (i + step) % size) for i in range(size)])


def after(value, *earlier):
    return lax.optimization_barrier((value, *earlier))[0]


def rows_kernel(me, scale_gate, scale_up, gate, up, out):
    first = (pl.program_id(0) + me[0]) % 4 * 5
    for at, scales, codes in ((0, scale_gate, gate), (1024, scale_up, up)):
        for i in range(5):
            for j in range(8):
                rows = pl.ds(i * 64, 64)
                value = codes[rows, pl.ds(j * QB, QB)].astype(F32) * scales[(first + i) // 2, j]
                out[rows, pl.ds(at + j * QB, QB)] = value.astype(BF)


def delta_rows(me, scale_gate, scale_up, gate, up):
    rows = pl.BlockSpec((320, 1024), lambda k, me: ((k + me[0]) % 4, 0))
    scalars = pl.BlockSpec(memory_space=pltpu.SMEM)
    return pl.pallas_call(
        rows_kernel,
        out_shape=jax.ShapeDtypeStruct((1280, 2048), BF),
        grid_spec=pltpu.PrefetchScalarGridSpec(
            num_scalar_prefetch=1,
            grid=(4,),
            in_specs=[scalars, scalars, rows, rows],
            out_specs=pl.BlockSpec((320, 2048), lambda k, me: (k, 0)),
        ),
        cost_estimate=pl.CostEstimate(flops=2621440, bytes_accessed=10485760, transcendentals=0),
        name="delta_rows",
    )(me, scale_gate, scale_up, gate, up)


def cols_kernel(scales, codes, out):
    j = pl.program_id(0)
    for i in range(8):
        rows = pl.ds(i * QB, QB)
        out[:, rows] = (codes[rows, :].astype(F32) * scales[i, j]).astype(BF).T


def delta_cols(codes, scales):
    return pl.pallas_call(
        cols_kernel,
        out_shape=jax.ShapeDtypeStruct((1280, 1024), BF),
        grid=(10,),
        in_specs=[
            pl.BlockSpec(memory_space=pltpu.SMEM),
            pl.BlockSpec((1024, QB), lambda j: (0, j)),
        ],
        out_specs=pl.BlockSpec((QB, 1024), lambda j: (j, 0)),
        cost_estimate=pl.CostEstimate(flops=1310720, bytes_accessed=5242880, transcendentals=0),
        name="delta_cols",
    )(scales, codes)


def sum_kernel(me, delta, *pieces_and_out):
    *pieces, out = pieces_and_out
    at = 0
    for piece in pieces:
        for k in range(0, piece.shape[0], 32):
            block = (me[0] + at // 320) % 4 * 320
            rows = pl.ds(pl.multiple_of(block + at % 320, 32), 32)
            base = piece[pl.ds(k, 32), :]
            out[rows, :] = (delta[rows, :].astype(F32) + base.astype(F32)).astype(BF)
            at += 32


def base_added(me, delta, *pieces):
    whole = pl.BlockSpec(memory_space=pltpu.VMEM)
    return pl.pallas_call(
        sum_kernel,
        out_shape=jax.ShapeDtypeStruct((1280, 1024), BF),
        in_specs=[pl.BlockSpec(memory_space=pltpu.SMEM)] + [whole] * (1 + len(pieces)),
        out_specs=whole,
        compiler_params=pltpu.CompilerParams(vmem_limit_bytes=24 * 2**20),
        cost_estimate=pl.CostEstimate(flops=1310720, bytes_accessed=7864320, transcendentals=0),
        name="base_added",
    )(me, delta, *pieces)


def near(value, axis):
    return shift(value, axis, -1), shift(value, axis, 1)


def far(ahead, behind, axis):
    half = ahead.shape[0] // 2
    return shift(behind[:half], axis, 1), shift(ahead[half:], axis, -1)


def scatter_first(part, half, axis):
    sent = part(2, (0, half)).astype(BF), part(2, (half, half)).astype(BF)
    sent = lax.optimization_barrier(sent)
    return sent, (shift(sent[0], axis, 1), shift(sent[1], axis, -1))


def scatter_second(part, got, axis):
    half = got[0].shape[0]
    first, second = (got[0].astype(F32), got[1].astype(F32))
    rest = ((0, 0),) * (first.ndim - 1)
    ahead = part(1, (0, 2 * half)) + jnp.pad(first, ((0, half),) + rest)
    behind = part(3, (0, 2 * half)) + jnp.pad(second, ((half, 0),) + rest)
    sent = lax.optimization_barrier((ahead.astype(BF), behind.astype(BF)))
    return sent, (shift(sent[0], axis, 1), shift(sent[1], axis, -1))


def scatter_sum(part, got):
    whole = part(0, (0, got[0].shape[0]))
    return whole + got[0].astype(F32) + got[1].astype(F32)


def from_zero(pieces, me):
    return [lax.select_n((me * 3 + k) % 4, *pieces) for k in range(4)]


def local(
    normed,
    base_gate,
    base_up,
    base_down,
    codes_gate,
    codes_up,
    codes_down,
    scale_gate,
    scale_up,
    scale_down,
):
    y, zh = lax.axis_index(Y), lax.axis_index(ZH)

    me = zh.reshape(1).astype(jnp.int32)

    own = normed.reshape(4, 16, 320)

    def kept_by(step):
        return lax.dynamic_index_in_dim(own, (y + step) % 4, 0, keepdims=False)

    ahead, behind = shift(kept_by(3), Y, -1), shift(kept_by(1), Y, 1)
    mine = jnp.concatenate((kept_by(0), ahead, behind, shift(kept_by(2), Y, 2)), 1)
    base = after(jnp.concatenate((base_gate, base_up), 1), mine)
    base_near = near(base, Y)
    ahead, behind = near(own, ZH)
    feats = jnp.concatenate((own, ahead, shift(own, ZH, 2), behind), 2)
    feats = jnp.concatenate((feats, mine[None]), 0)[:, None]
    feats = jnp.concatenate((feats, shift(feats, ZL, 1)), 1)
    codes_gate, codes_up = after((codes_gate, codes_up), feats)
    delta = delta_rows(me, scale_gate, scale_up, codes_gate, codes_up)
    ahead, behind = near(feats, X)
    ahead, behind = after((ahead, behind), delta)
    first, second = shift(behind[:, :1], X, 1), shift(ahead[:, 1:], X, -1)
    first, second, base_near = lax.optimization_barrier((first, second, base_near))
    base_sent = lax.optimization_barrier((base_near[1][:160], base_near[0][160:]))
    base_far = shift(base_sent[0], Y, 1), shift(base_sent[1], Y, -1)
    down_own = after(base_down.T, first)
    down_near = near(down_own, ZH)
    first, second = after((first, second), *base_sent)
    feats = jnp.concatenate((feats, ahead, first, second, behind), 1)
    feats = jnp.concatenate((feats, shift(feats, CORE, 1)), 1)
    feats, base_near = lax.optimization_barrier((feats.reshape(1280, 1280), base_near))
    mine, feats = feats[1024:], feats[:1024]

    def delta_term(step, rows):
        at = (y + step) % 4 * 256 + rows[0]
        return dot(lax.dynamic_slice_in_dim(feats, at, rows[1], 0), delta)

    base = lax.optimization_barrier(jnp.concatenate((base, *base_near), 0))
    base_part = lax.optimization_barrier(dot(mine[:, :960], base))
    base_far = after(base_far, base_part)
    base_part += dot(mine[:, 960:1120], base_far[0]) + dot(mine[:, 1120:], base_far[1])
    base_part = lax.optimization_barrier(base_part)

    def base_term(step, rows):
        at = (zh + step) % 4 * 64 + rows[0]
        return lax.dynamic_slice_in_dim(base_part, at, rows[1], 0)

    base_sent, base_got = scatter_first(base_term, 32, ZH)
    feats = after(feats, base_sent)
    delta_sent, delta_got = scatter_first(delta_term, 128, Y)
    feats, base_got, down_near = after((feats, base_got, down_near), delta_sent)
    base_sent, base_got = scatter_second(base_term, base_got, ZH)
    ready = lax.optimization_barrier([delta_term(k, (0, 256)) for k in (1, 3)])
    delta_got = after(delta_got, base_sent, *down_near, *ready)
    delta_sent, delta_got = scatter_second(lambda k, rows: ready[k // 2], delta_got, Y)
    base_got = after(base_got, delta_sent)
    total = scatter_sum(base_term, base_got).astype(BF)
    ahead, behind = near(total, ZH)
    feats, codes_down = after((feats, codes_down), total)
    delta_down = delta_cols(codes_down, scale_down)
    delta_own = lax.optimization_barrier(delta_term(0, (0, 256)))
    ahead, behind = after((ahead, behind), delta_down, delta_own)
    opposite = far(ahead, behind, ZH)
    delta_got, down_near = after((delta_got, down_near), ahead, behind)
    down_far = far(*down_near, ZH)
    opposite = after(opposite, *delta_got)
    opposite = jnp.pad(opposite[0], ((0, 32), (0, 0))) + jnp.pad(opposite[1], ((32, 0), (0, 0)))
    total = jnp.concatenate(from_zero((total, ahead, opposite, behind), zh), 0).astype(F32)
    total += delta_own + delta_got[0].astype(F32) + delta_got[1].astype(F32)

    hidden = (jax.nn.silu(total[:, :1024]) * total[:, 1024:]).astype(BF)
    ahead, behind = near(hidden, Y)
    opposite = far(ahead, behind, Y)
    down_far = after(down_far, ahead, behind)
    w_down = base_added(me, delta_down, down_own, down_near[0], *down_far, down_near[1])
    opposite = after(opposite, w_down)
    def down(pieces, half):
        rows = jnp.concatenate([p[half * 128 : half * 128 + 128] for p in pieces], 0)
        return dot(rows, w_down.T)

    def exchanged(pieces):
        sent = lax.optimization_barrier(down(pieces, 1).astype(BF))
        other = shift(sent, CORE, 1)
        kept = lax.optimization_barrier(down(pieces, 0))
        return kept, after(other, kept)

    kept, other = exchanged((hidden, ahead, behind))
    opposite = after(opposite, kept)
    far_kept, far_other = exchanged((jnp.concatenate(opposite, 0),))
    whole = (kept + other.astype(F32)).astype(BF)
    far_whole = (far_kept + far_other.astype(F32)).astype(BF)
    whole = jnp.concatenate((whole[:256], far_whole, whole[256:]), 0)
    whole = lax.optimization_barrier(whole)
    whole = whole.reshape(4, 4, 2, 16, 1280)

    def for_x(step, rows):
        piece = whole[:, step, rows[0] : rows[0] + rows[1]]
        return piece.transpose(1, 0, 2, 3).astype(F32)

    sent, got = scatter_first(for_x, 1, X)
    sent, got = scatter_second(for_x, got, X)
    mine = scatter_sum(for_x, got)
    theirs = shift(mine[1].astype(BF), ZL, 1)
    mine = (mine[0] + theirs.astype(F32)).astype(BF)
    return jnp.concatenate(from_zero([mine[k] for k in range(4)], y), 0)


def solution(mesh):
    fine = Mesh(mesh.devices.reshape(4, 4, 2, 4, 2), (Y, ZH, ZL, X, CORE))
    rows, cols = P((Y, ZH), TENSOR), P(TENSOR, (Y, ZH))
    in_specs = (cols, rows, rows, cols, rows, rows, cols, rows, rows, cols)
    return jax.shard_map(local, mesh=fine, in_specs=in_specs, out_specs=cols, check_vma=False)
```
